32 devices in a mesh: dp: 4 (over y, core), vocab: 8 (over z, x).
Axes of the slice: x: 2, y: 2, z: 4, core: 2. Of those that a mesh axis runs over, the one named last changes fastest.
Arguments:
- hidden_states: bfloat16 [4, 1024, 8192], P(None, 'dp', 'vocab'), may hold values from -400 to 400
- exit_layers: int32 [16, 2], P('dp'), may hold values from 0 to 3, all different within a row
- targets: int32 [1024], P('dp'), may hold values from 0 to 2047
- norm_gain: bfloat16 [8192], replicated, may hold values from 0.25 to 1.75
- exit_scale: float32 [2], replicated, may hold values from 0.5 to 2
- unembedding: bfloat16 [8192, 2048], P(None, 'vocab'), may hold values from -3 to 3
Outputs:
- weight_grad: float32 [8192, 2048], P('dp', 'vocab')
- mean_loss: float32 [], replicated
The draws below stay inside these ranges and needn't reach their ends.
Inputs may be any that keep to these rules, and one draw needn't show every extreme that they name: `exit_layers`: each row of 64 tokens names 2 different layers, and every layer is named by some row.
All inputs are finite; a program needn't handle non-finite values.
Results may differ from the reference program's by a relative error of at most 0.013.
Values may be sent and summed in bfloat16 or wider, within the bound.
No kernel may reach another device: no remote copies, remote signals or barrier semaphores. Data moves between devices by JAX's collectives and lax.ppermute only.
A program may use at most 128 MiB of HBM per device.

```python
import math
import jax
import jax.numpy as jnp
from jax import lax

D = 8192
VOCAB_DEV = 256
LAYERS = 4
EXITS = 2
SEQ = 64
TOK_DEV = 256
TOKENS = 1024
ROWS = 16
VOCAB = 2048
N_DP = 4


def pair_columns(key):
    first_cols = jax.random.permutation(jax.random.fold_in(key, 103), VOCAB)[:8]
    return (first_cols, (first_cols + VOCAB_DEV) % VOCAB)


def align_size():
    return min(max(3.0 / math.sqrt(D), 190.0 / D), 2.95)


def sign_columns(key):
    flips = jax.random.randint(jax.random.fold_in(key, 104), (8, D), 0, 2).astype(jnp.float32)
    return 2.0 * flips - 1.0


def make_unembed(key):
    base_field = jnp.clip(jax.random.normal(jax.random.fold_in(key, 101), (D, VOCAB), jnp.float32), -6.0, 6.0)
    weights = base_field * (3.0 / math.sqrt(D))
    first_cols, second_cols = pair_columns(key)
    special = sign_columns(key).T * align_size()
    weights = weights.at[:, first_cols].set(special)
    weights = weights.at[:, second_cols].set(0.98 * special + 0.1 * weights[:, second_cols])
    return jnp.clip(weights, -3.0, 3.0)


def draw_unembedding(key, part):
    return make_unembed(key).astype(jnp.bfloat16)


def draw_hidden_states(key, part):
    base_field = jnp.clip(jax.random.normal(jax.random.fold_in(key, 111), (LAYERS, TOKENS, D), jnp.float32), -5.0, 5.0)
    col_scale = 1.0 + 2.0 * jnp.arange(D, dtype=jnp.float32) / D
    row_scale = jnp.exp(jax.random.uniform(jax.random.fold_in(key, 113), (LAYERS, TOKENS, 1), jnp.float32, 0.0, math.log(10.0)))
    field = base_field * col_scale
    weights = make_unembed(key)
    positions = jnp.arange(TOKENS, dtype=jnp.int32)
    place = positions.astype(jnp.float32) / TOKENS
    lift = 0.95 * place
    token_cols = jax.random.randint(jax.random.fold_in(key, 116), (TOKENS,), 0, VOCAB)
    toward = weights.T[token_cols] * (math.sqrt(D) / 3.0)
    field = jnp.sqrt(1.0 - lift * lift)[None, :, None] * field + lift[None, :, None] * toward[None]
    is_aligned = positions % 37 == 3
    pair_slot = positions % 8
    strength = 0.7 + 0.15 * (positions // 37 % 3).astype(jnp.float32)
    aligned = sign_columns(key)[pair_slot]
    mixed = strength[:, None] * aligned + jnp.sqrt(1.0 - strength * strength)[:, None] * base_field
    field = jnp.where(is_aligned[None, :, None], mixed, field)
    return jnp.clip(field * row_scale, -400.0, 400.0).astype(jnp.bfloat16)


def set_ends(array, own_key, low, high):
    spot = [jax.random.randint(jax.random.fold_in(own_key, axis), (), 0, length) for axis, length in enumerate(array.shape)]
    main_axis = array.shape.index(max(array.shape))
    next_to = spot[:main_axis] + [(spot[main_axis] + 1) % array.shape[main_axis]] + spot[main_axis + 1:]
    return array.at[tuple(spot)].set(low).at[tuple(next_to)].set(high)


def choose_distinct(stream_key, rows, number_of, top, lift):
    sequence = jax.random.permutation(jax.random.fold_in(stream_key, 1), number_of)
    boost = sequence
    for power in range(3):
        boost = boost * boost // number_of
    boost = boost * lift // number_of
    lots = jax.random.randint(jax.random.fold_in(stream_key, 2), (rows, number_of), 0, 4096) + boost
    fixed_rows = jax.random.permutation(jax.random.fold_in(stream_key, 3), rows)[jnp.arange(number_of) % rows]
    lots = jnp.where(jnp.arange(rows)[:, None] == fixed_rows[None, :], 1 << 14, lots)
    score = lots * number_of + jnp.arange(number_of)
    return lax.top_k(score.astype(jnp.int32), top)[1].astype(jnp.int32)


def setup_inputs(seed: int = 0) -> dict:
    key_of = jax.random.split(jax.random.key(seed), 7)
    hidden_states = draw_hidden_states(jax.random.fold_in(key_of[6], 71), 0)
    exit_layers = choose_distinct(key_of[1], ROWS, LAYERS, EXITS, 0)
    targets = set_ends(jax.random.randint(key_of[2], (TOKENS,), 0, VOCAB), jax.random.fold_in(key_of[2], 1), 0, VOCAB - 1).astype(jnp.int32)
    norm_gain = jnp.clip(1.0 + 0.15 * jax.random.normal(key_of[3], (D,), jnp.float32), 0.25, 1.75).astype(jnp.bfloat16)
    exit_scale = jnp.clip(jnp.exp(jax.random.uniform(key_of[4], (EXITS,), jnp.float32, math.log(0.5), math.log(2.0))), 0.5, 2.0)
    unembedding = draw_unembedding(jax.random.fold_in(key_of[6], 71), 0)
    return {"hidden_states": hidden_states, "exit_layers": exit_layers, "targets": targets, "norm_gain": norm_gain, "exit_scale": exit_scale, "unembedding": unembedding}


norm_eps = 1e-05

def reference(hidden_states, exit_layers, targets, norm_gain, exit_scale, unembedding):
    positions = jnp.arange(TOKENS, dtype=jnp.int32)
    row_layers = jnp.repeat(exit_layers, SEQ, axis=0)
    selected = jnp.stack([hidden_states[row_layers[:, index], positions] for index in range(EXITS)])
    values = selected.astype(jnp.float32)
    mean_sq = lax.optimization_barrier(jnp.mean(values * values, axis=-1, keepdims=True))
    normed = (values * lax.rsqrt(mean_sq + norm_eps) * norm_gain.astype(jnp.float32)).astype(jnp.bfloat16)
    grouped = normed.reshape(EXITS, N_DP, TOK_DEV, D).transpose(1, 0, 2, 3).reshape(N_DP, EXITS * TOK_DEV, D)
    group_targets = jnp.tile(targets.reshape(N_DP, TOK_DEV), (1, EXITS))
    scale_rows = jnp.repeat(exit_scale, TOK_DEV)
    columns = jnp.arange(VOCAB, dtype=jnp.int32)

    def one_group(state_pair, inputs):
        grad_total, loss_total = state_pair
        group_rows, labels = inputs
        logits = jnp.dot(group_rows, unembedding, preferred_element_type=jnp.float32)
        row_top = lax.optimization_barrier(jnp.max(logits, axis=-1))
        log_total = row_top + jnp.log(lax.optimization_barrier(jnp.sum(jnp.exp(logits - row_top[:, None]), axis=-1)))
        is_target = labels[:, None] == columns[None, :]
        target_logit = lax.optimization_barrier(jnp.sum(jnp.where(is_target, logits, 0.0), axis=-1))
        loss_total = loss_total + jnp.sum(scale_rows * (log_total - target_logit))
        logit_grad = (scale_rows[:, None] * (jnp.exp(logits - log_total[:, None]) - is_target.astype(jnp.float32))).astype(jnp.bfloat16)
        partial_grad = lax.dot_general(group_rows, logit_grad, (((0,), (0,)), ((), ())), preferred_element_type=jnp.float32)
        rounded = lax.optimization_barrier(partial_grad.astype(jnp.bfloat16))
        return ((grad_total + rounded.astype(jnp.float32), loss_total), None)
    start_state = (jnp.zeros((D, VOCAB), jnp.float32), jnp.zeros((), jnp.float32))
    final_state, ignored = lax.scan(one_group, start_state, (grouped, group_targets))
    return (final_state[0], final_state[1] / TOKENS)
```

```python
import functools

import jax
import jax.numpy as jnp
from jax import lax
from jax.experimental import pallas as pl
from jax.experimental.pallas import tpu as pltpu
from jax.sharding import PartitionSpec as P

norm_eps = 1e-05
f32, bf16 = jnp.float32, jnp.bfloat16
vmem_bytes = 32 * 1024 * 1024
bar = lax.optimization_barrier


def params():
    return pltpu.CompilerParams(vmem_limit_bytes=vmem_bytes)


def whole(shape):
    return pl.BlockSpec(shape, lambda *_: (0,) * len(shape))


def select_kernel(exit_index, row_len, layers_ref, hidden_ref, out_ref, sems):
    rows = layers_ref.shape[0]
    copies = []
    for r in range(rows):
        span = pl.ds(r * row_len, row_len)
        copies.append(
            pltpu.make_async_copy(
                hidden_ref.at[layers_ref[r, exit_index], span], out_ref.at[span], sems.at[r]
            )
        )
    for copy in copies:
        copy.start()
    for copy in copies:
        copy.wait()


def select(hidden, exit_layers, exit_index):
    _, tokens, width = hidden.shape
    rows = exit_layers.shape[0]
    return pl.pallas_call(
        functools.partial(select_kernel, exit_index, tokens // rows),
        out_shape=jax.ShapeDtypeStruct((tokens, width), hidden.dtype),
        in_specs=[pl.BlockSpec(memory_space=pltpu.SMEM), pl.BlockSpec(memory_space=pl.ANY)],
        out_specs=pl.BlockSpec(memory_space=pl.ANY),
        scratch_shapes=[pltpu.SemaphoreType.DMA((rows,))],
        compiler_params=params(),
        name="select_rows",
    )(exit_layers, hidden)


def piece_kernel(first, *refs):
    if first:
        _, piece, gain, weights, acc_out, ss_out, scaled_out = refs
    else:
        _, piece, gain, weights, acc, ss, _, acc_out, ss_out, scaled_out = refs
    x = piece[...].astype(f32)
    scaled = (x * gain[...].astype(f32)).astype(bf16)
    scaled_out[...] = scaled
    logits = jnp.dot(scaled, weights[...], preferred_element_type=f32)
    lanes = ss_out.shape[1]
    square = x * x
    sums = square[:, :lanes]
    for start in range(lanes, x.shape[1], lanes):
        sums = sums + square[:, start : start + lanes]
    if first:
        acc_out[...] = logits
        ss_out[...] = sums
    else:
        acc_out[...] = acc[...] + logits
        ss_out[...] = ss[...] + sums


def add_piece(state, block, piece, gain_row, unembedding):
    rows, width = piece.shape
    full, vocab = unembedding.shape
    lanes = min(128, width)
    first = state is None
    in_specs = [
        whole((rows, width)),
        pl.BlockSpec((1, width), lambda i, b: (0, b[0])),
        pl.BlockSpec((width, vocab), lambda i, b: (b[0], 0)),
    ]
    if not first:
        in_specs += [whole((rows, vocab)), whole((rows, lanes)), pl.BlockSpec(memory_space=pl.ANY)]
    return pl.pallas_call(
        functools.partial(piece_kernel, first),
        grid_spec=pltpu.PrefetchScalarGridSpec(
            num_scalar_prefetch=1,
            grid=(1,),
            in_specs=in_specs,
            out_specs=[
                whole((rows, vocab)),
                whole((rows, lanes)),
                pl.BlockSpec((rows, width), lambda i, b: (0, b[0])),
            ],
        ),
        out_shape=[
            jax.ShapeDtypeStruct((rows, vocab), f32),
            jax.ShapeDtypeStruct((rows, lanes), f32),
            jax.ShapeDtypeStruct((rows, full), bf16),
        ],
        input_output_aliases={} if first else {4: 0, 5: 1, 6: 2},
        compiler_params=params(),
        name="piece",
    )(block, piece, gain_row, unembedding, *(() if first else state))


def row_scale(ss, full):
    mean_sq = jnp.sum(ss, axis=1, keepdims=True) * (1.0 / full)
    return lax.rsqrt(mean_sq + norm_eps)


def target_mask(offset, target_col, shape):
    ids = lax.broadcasted_iota(jnp.int32, shape, 1) + offset
    return ids == target_col


def stats_kernel(full, offset, acc, ss, targets, logits_out, stats_out):
    logits = acc[...] * row_scale(ss[...], full)
    logits_out[...] = logits
    hit = target_mask(offset[0], targets[...], logits.shape)
    target = jnp.sum(jnp.where(hit, logits, 0.0), axis=1, keepdims=True)
    top = jnp.max(logits, axis=1, keepdims=True)
    total = jnp.sum(jnp.exp(logits - top), axis=1, keepdims=True)
    lane = lax.broadcasted_iota(jnp.int32, (logits.shape[0], 128), 1)
    packed = jnp.where(lane == 0, top, jnp.where(lane == 1, total, target))
    stats_out[...] = packed.T[:8, :]


def row_stats(offset, acc, ss, target_col, full):
    rows, vocab = acc.shape
    return pl.pallas_call(
        functools.partial(stats_kernel, full),
        grid_spec=pltpu.PrefetchScalarGridSpec(
            num_scalar_prefetch=1,
            grid=(1,),
            in_specs=[whole(acc.shape), whole(ss.shape), whole(target_col.shape)],
            out_specs=[whole((rows, vocab)), whole((8, rows))],
        ),
        out_shape=[
            jax.ShapeDtypeStruct((rows, vocab), f32),
            jax.ShapeDtypeStruct((8, rows), f32),
        ],
        compiler_params=params(),
        name="row_stats",
    )(offset, acc, ss, target_col)


def merge_kernel(a, b, out):
    top_a, top_b = a[0:1, :], b[0:1, :]
    top = jnp.maximum(top_a, top_b)
    total = a[1:2, :] * jnp.exp(top_a - top) + b[1:2, :] * jnp.exp(top_b - top)
    target = a[2:3, :] + b[2:3, :]
    row = lax.broadcasted_iota(jnp.int32, out.shape, 0)
    out[...] = jnp.where(row == 0, top, jnp.where(row == 1, total, target))


def merge(a, b):
    return pl.pallas_call(
        merge_kernel,
        out_shape=jax.ShapeDtypeStruct(a.shape, f32),
        compiler_params=params(),
        name="merge_stats",
    )(a, b)


def grad_kernel(full, offset, logits, ss, targets, stats, scale, grad_out, loss_out):
    exits = len(ss)
    tokens = ss[0].shape[0]
    log_total = stats[0:1, :] + jnp.log(stats[1:2, :])
    token_loss = log_total - stats[2:3, :]
    loss = jnp.zeros((1, 1), f32)
    for e in range(exits):
        part = token_loss[:, e * tokens : (e + 1) * tokens]
        loss = loss + scale[e] * jnp.sum(part, axis=1, keepdims=True)
        rows_log = jnp.broadcast_to(log_total[:, e * tokens : (e + 1) * tokens], (128, tokens))
        col = rows_log.T[:, 0:1]
        values = logits[e][...]
        hit = target_mask(offset[0], targets[...], values.shape)
        soft = jnp.exp(values - col) - jnp.where(hit, 1.0, 0.0)
        factor = row_scale(ss[e][...], full) * scale[e]
        grad_out[e * tokens : (e + 1) * tokens, :] = (soft * factor).astype(bf16)
    loss_out[...] = jnp.broadcast_to(loss, loss_out.shape)


def row_grads(offset, logits, ss, target_col, stats, exit_scale, full):
    exits = len(logits)
    tokens, vocab = logits[0].shape

    def body(off, *refs):
        grad_kernel(
            full, off, refs[:exits], refs[exits : 2 * exits], *refs[2 * exits :]
        )

    return pl.pallas_call(
        body,
        grid_spec=pltpu.PrefetchScalarGridSpec(
            num_scalar_prefetch=1,
            grid=(1,),
            in_specs=[whole(a.shape) for a in (*logits, *ss, target_col, stats)]
            + [pl.BlockSpec(memory_space=pltpu.SMEM)],
            out_specs=[whole((exits * tokens, vocab)), whole((8, 128))],
        ),
        out_shape=[
            jax.ShapeDtypeStruct((exits * tokens, vocab), bf16),
            jax.ShapeDtypeStruct((8, 128), f32),
        ],
        compiler_params=params(),
        name="row_grads",
    )(offset, *logits, *ss, target_col, stats, exit_scale)


def share_kernel(exits, n_add, *refs):
    scaled = refs[1 : 1 + exits]
    grads = refs[1 + exits]
    added = refs[2 + exits : 2 + exits + n_add]
    out = refs[-1]
    tokens = scaled[0].shape[0]
    total = None
    for e in range(exits):
        part = lax.dot_general(
            scaled[e][...],
            grads[e * tokens : (e + 1) * tokens, :],
            (((0,), (0,)), ((), ())),
            preferred_element_type=f32,
        )
        total = part if total is None else total + part
    for ref in added:
        total = total + ref[...].astype(f32)
    out[...] = total.astype(out.dtype)


def grad_share(share, n_share, scaled, grads, added, dtype):
    exits = len(scaled)
    tokens, full = scaled[0].shape
    vocab = grads.shape[1]
    height = full // n_share
    tile = min(512, height)
    steps = height // tile
    return pl.pallas_call(
        functools.partial(share_kernel, exits, len(added)),
        grid_spec=pltpu.PrefetchScalarGridSpec(
            num_scalar_prefetch=1,
            grid=(steps,),
            in_specs=[
                pl.BlockSpec((tokens, tile), lambda i, s: (0, s[0] * steps + i)) for _ in scaled
            ]
            + [whole(grads.shape)]
            + [pl.BlockSpec((tile, vocab), lambda i, s: (i, 0)) for _ in added],
            out_specs=pl.BlockSpec((tile, vocab), lambda i, s: (i, 0)),
        ),
        out_shape=jax.ShapeDtypeStruct((height, vocab), dtype),
        compiler_params=params(),
        name="grad_share",
    )(share, *scaled, grads, *added)


def flip(axis, bit):
    return [(i, i ^ bit) for i in range(lax.axis_size(axis))]


def per_device(hidden_states, exit_layers, targets, norm_gain, exit_scale, unembedding):
    exits = exit_layers.shape[1]
    tokens = hidden_states.shape[1]
    full, vocab_local = unembedding.shape
    n_vocab, n_dp = lax.axis_size("vocab"), lax.axis_size("dp")
    ring_size = n_vocab // 2
    here = lax.axis_index("vocab")
    ring_at, side = here // 2, here % 2
    ring = [(j, (j + 2) % n_vocab) for j in range(n_vocab)]
    pair = flip("vocab", 1)
    gain_row = norm_gain.reshape(1, full)
    target_col = targets.reshape(tokens, 1)
    offset = (here * vocab_local).reshape(1).astype(jnp.int32)

    state = [None] * exits
    current = [select(hidden_states, exit_layers, e) for e in range(exits)]
    crossed = None
    for step in range(ring_size):
        owner = lax.rem(ring_at - step + ring_size, ring_size) * 2
        own_block = (owner + side).reshape(1).astype(jnp.int32)
        cross_block = (owner + 1 - side).reshape(1).astype(jnp.int32)
        last = step == ring_size - 1
        crossing, coming = [], []
        for e in range(exits):
            piece = current[e]
            if crossed is not None:
                piece, crossed[e] = bar((piece, crossed[e]))
            if last and step > 0 and e >= exits // 2:
                crossing.append(lax.ppermute(crossed[e], "vocab", ring))
            else:
                crossing.append(lax.ppermute(piece, "vocab", pair))
            if not last:
                coming.append(lax.ppermute(piece, "vocab", ring))
            current[e] = piece
        for e in range(exits):
            if crossed is not None:
                state[e] = add_piece(state[e], crossed_block, crossed[e], gain_row, unembedding)
            state[e] = add_piece(state[e], own_block, current[e], gain_row, unembedding)
        crossed, crossed_block, current = crossing, cross_block, coming
    for e in range(exits):
        state[e] = add_piece(state[e], crossed_block, crossed[e], gain_row, unembedding)

    logits, stats = [], []
    for acc, ss, _ in state:
        part, row = row_stats(offset, acc, ss, target_col, full)
        logits.append(part)
        stats.append(row)
    stats = jnp.concatenate(stats, axis=1)
    bit = 1
    while bit < n_vocab:
        stats = merge(stats, lax.ppermute(stats, "vocab", flip("vocab", bit)))
        bit *= 2
    grads, loss = row_grads(
        offset, logits, [s[1] for s in state], target_col, stats, exit_scale, full
    )

    scaled = [s[2] for s in state]
    group = lax.axis_index("dp")
    high, low = group // 2, group % 2

    def share_of(high_flip, low_index):
        return ((high ^ high_flip) * 2 + low_index).reshape(1).astype(jnp.int32)

    held = {}
    n_high = n_dp // 2
    for high_flip in reversed(range(n_high)):
        away = grad_share(share_of(high_flip, 1 - low), n_dp, scaled, grads, (), bf16)
        came = lax.ppermute(away, "dp", flip("dp", 1))
        held[high_flip] = grad_share(
            share_of(high_flip, low), n_dp, scaled, grads, (came,), bf16 if high_flip else f32
        )
    bit = 1
    while bit < n_high:
        kept = {}
        for h in sorted(held, reverse=True):
            if not h & bit:
                came = lax.ppermute(held[h | bit], "dp", flip("dp", 2 * bit))
                total = held[h].astype(f32) + came.astype(f32)
                kept[h] = total.astype(bf16) if h else total
        held = kept
        bit *= 2
    weight_grad = held[0]
    bit = 1
    while bit < n_dp:
        loss = loss + lax.ppermute(loss, "dp", flip("dp", bit))
        bit *= 2
    mean_loss = loss[0, 0] / (tokens * n_dp)
    return (weight_grad, mean_loss)


def solution(mesh):
    in_specs = (P(None, "dp", "vocab"), P("dp", None), P("dp"), P(), P(), P(None, "vocab"))
    out_specs = (P("dp", "vocab"), P())
    return jax.shard_map(
        per_device, mesh=mesh, in_specs=in_specs, out_specs=out_specs, check_vma=False
    )
```

```python
import functools

import jax
import jax.numpy as jnp
from jax import lax
from jax.experimental import pallas as pl
from jax.experimental.pallas import tpu as pltpu
from jax.sharding import PartitionSpec as P

norm_eps = 1e-05
f32, bf16 = jnp.float32, jnp.bfloat16
vmem_bytes = 16 * 1024 * 1024
bar = lax.optimization_barrier
smem_spec = pl.BlockSpec(memory_space=pltpu.SMEM)
hbm_spec = pl.BlockSpec(memory_space=pltpu.HBM)
vmem_spec = pl.BlockSpec(memory_space=pltpu.VMEM)


def call(kernel, name, out_shape, in_specs, out_specs, **more):
    return pl.pallas_call(
        kernel,
        name=name,
        out_shape=out_shape,
        in_specs=in_specs,
        out_specs=out_specs,
        compiler_params=pltpu.CompilerParams(vmem_limit_bytes=vmem_bytes),
        **more,
    )


def select_kernel(exit_index, row_len, layers_ref, hidden_ref, out_ref, sems):
    copies = []
    for r in range(layers_ref.shape[1]):
        span = pl.ds(r * row_len, row_len)
        source = hidden_ref.at[layers_ref[exit_index, r], span]
        copies.append(pltpu.make_async_copy(source, out_ref.at[span], sems.at[r]))
    for copy in copies:
        copy.start()
    for copy in copies:
        copy.wait()


def select(hidden, layers, exit_index):
    _, tokens, width = hidden.shape
    rows = layers.shape[1]
    return call(
        functools.partial(select_kernel, exit_index, tokens // rows),
        "select_rows",
        jax.ShapeDtypeStruct((tokens, width), hidden.dtype),
        [smem_spec, hbm_spec],
        pl.BlockSpec(memory_space=pl.ANY),
        scratch_shapes=[pltpu.SemaphoreType.DMA((rows,))],
    )(layers, hidden)


def add_blocks(ids, pieces, spans, gain, unembedding, accs, sums, scaled_out, weight_buf, scaled_buf, in_sems, out_sems):
    width = pieces[0].shape[1]
    n = len(pieces)
    loads, stores = [], []
    for p in range(n):
        rows = unembedding.at[pl.ds(pl.multiple_of(ids[p] * width, width), width)]
        loads.append(pltpu.make_async_copy(rows, weight_buf.at[p], in_sems.at[p]))
        loads[p].start()
    for p in range(n):
        x = pieces[p][...].astype(f32)
        scaled_buf[p] = (x * gain[pl.ds(ids[p], 1), :]).astype(bf16)
        stores.append(
            pltpu.make_async_copy(scaled_buf.at[p], scaled_out.at[ids[p], spans[p]], out_sems.at[p])
        )
        stores[p].start()
        square = x * x
        lanes = min(128, width)
        total = square[:, :lanes]
        for start in range(lanes, width, lanes):
            total = total + square[:, start : start + lanes]
        sums[p] = total
    for p in range(n):
        loads[p].wait()
        accs[p] = jnp.dot(scaled_buf[p], weight_buf[p], preferred_element_type=f32)
    for p in range(n):
        stores[p].wait()


def block_scratch(n, rows, width, vocab):
    return [
        pltpu.VMEM((n, width, vocab), bf16),
        pltpu.VMEM((n, rows, width), bf16),
        pltpu.SemaphoreType.DMA((n,)),
        pltpu.SemaphoreType.DMA((n,)),
    ]


def arrival_kernel(n, first, makes, exit_index, ids, *refs):
    pieces, refs = refs[:n], refs[n:]
    gain, unembedding = refs[:2]
    refs = refs[2:]
    if not first:
        acc, ss = refs[:2]
        refs = refs[2:]
    if not makes:
        refs = refs[1:]
    acc_out, ss_out, scaled_out = refs[:3]
    rows = pieces[0].shape[0]
    span = pl.ds(exit_index * rows, rows)
    accs, sums = [None] * n, [None] * n
    add_blocks(ids, pieces, [span] * n, gain, unembedding, accs, sums, scaled_out, *refs[3:])
    total, squares = accs[0], sums[0]
    for p in range(1, n):
        total, squares = total + accs[p], squares + sums[p]
    if not first:
        total, squares = total + acc[...], squares + ss[...]
    acc_out[...] = total
    ss_out[...] = squares


def arrival(state, scaled, exit_index, exits, ids, pieces, gain, unembedding):
    rows, width = pieces[0].shape
    full, vocab = unembedding.shape
    lanes = min(128, width)
    n = len(pieces)
    first, makes = state is None, scaled is None
    args = [ids, *pieces, gain, unembedding]
    specs = [smem_spec] + [vmem_spec] * (n + 1) + [hbm_spec]
    aliases = {}
    if not first:
        aliases = {len(args): 0, len(args) + 1: 1}
        args += list(state)
        specs += [vmem_spec, vmem_spec]
    if not makes:
        aliases[len(args)] = 2
        args.append(scaled)
        specs.append(hbm_spec)
    acc, ss, scaled = call(
        functools.partial(arrival_kernel, n, first, makes, exit_index),
        "arrival",
        [
            jax.ShapeDtypeStruct((rows, vocab), f32),
            jax.ShapeDtypeStruct((rows, lanes), f32),
            jax.ShapeDtypeStruct((full // width, exits * rows, width), bf16),
        ],
        specs,
        [vmem_spec, vmem_spec, hbm_spec],
        input_output_aliases=aliases,
        scratch_shapes=block_scratch(n, rows, width, vocab),
    )(*args)
    return (acc, ss), scaled


def target_mask(offset, targets, shape):
    return lax.broadcasted_iota(jnp.int32, shape, 1) + offset == targets[...]


def last_kernel(exits, full, ids, offset, *refs):
    pieces, refs = refs[:exits], refs[exits:]
    gain, unembedding = refs[:2]
    old_acc, old_ss, refs = refs[2 : 2 + exits], refs[2 + exits : 2 + 2 * exits], refs[2 + 2 * exits :]
    targets, _, logits_out, stats_out, scaled_out = refs[:5]
    rows = pieces[0].shape[0]
    spans = [pl.ds(e * rows, rows) for e in range(exits)]
    accs, sums = [None] * exits, [None] * exits
    add_blocks(ids, pieces, spans, gain, unembedding, accs, sums, scaled_out, *refs[5:])
    for e in range(exits):
        square_sum = jnp.sum(old_ss[e][...] + sums[e], axis=1, keepdims=True)
        scale = lax.rsqrt(square_sum * (1.0 / full) + norm_eps)
        logits = (old_acc[e][...] + accs[e]) * scale
        logits_out[spans[e], :] = logits
        hit = target_mask(offset[0], targets, logits.shape)
        target = jnp.sum(jnp.where(hit, logits, 0.0), axis=1, keepdims=True)
        top = jnp.max(logits, axis=1, keepdims=True)
        total = jnp.sum(jnp.exp(logits - top), axis=1, keepdims=True)
        lane = lax.broadcasted_iota(jnp.int32, (rows, 128), 1)
        packed = jnp.where(
            lane == 0, top, jnp.where(lane == 1, total, jnp.where(lane == 2, target, scale))
        )
        stats_out[:, e * rows : (e + 1) * rows] = packed.T[:8, :]


def last_blocks(states, scaled, ids, offset, pieces, targets, gain, unembedding):
    exits = len(pieces)
    rows, width = pieces[0].shape
    full, vocab = unembedding.shape
    args = [ids, offset, *pieces, gain, unembedding, *[s[0] for s in states], *[s[1] for s in states], targets, scaled]
    specs = [smem_spec] * 2 + [vmem_spec] * (exits + 1) + [hbm_spec] + [vmem_spec] * (2 * exits + 1) + [hbm_spec]
    return call(
        functools.partial(last_kernel, exits, full),
        "last_blocks",
        [
            jax.ShapeDtypeStruct((exits * rows, vocab), f32),
            jax.ShapeDtypeStruct((8, exits * rows), f32),
            jax.ShapeDtypeStruct(scaled.shape, bf16),
        ],
        specs,
        [vmem_spec, vmem_spec, hbm_spec],
        input_output_aliases={len(args) - 1: 2},
        scratch_shapes=block_scratch(exits, rows, width, vocab),
    )(*args)


def merge_kernel(a, b, out):
    top_a, top_b = a[0:1, :], b[0:1, :]
    top = jnp.maximum(top_a, top_b)
    total = a[1:2, :] * jnp.exp(top_a - top) + b[1:2, :] * jnp.exp(top_b - top)
    target = a[2:3, :] + b[2:3, :]
    row = lax.broadcasted_iota(jnp.int32, out.shape, 0)
    out[...] = jnp.where(row == 0, top, jnp.where(row == 1, total, target))


def merge(a, b):
    shape = jax.ShapeDtypeStruct(a.shape, f32)
    return call(merge_kernel, "merge_stats", shape, [vmem_spec] * 2, vmem_spec)(a, b)


def grad_kernel(exits, offset, logits, own_stats, stats, targets, exit_scale, grad_out, loss_out):
    rows = logits.shape[0] // exits
    loss = jnp.zeros((1, 1), f32)
    for e in range(exits):
        cols = slice(e * rows, (e + 1) * rows)
        log_total = stats[0:1, cols] + jnp.log(stats[1:2, cols])
        token_loss = log_total - stats[2:3, cols]
        loss = loss + exit_scale[e] * jnp.sum(token_loss, axis=1, keepdims=True)
        factor = own_stats[3:4, cols] * exit_scale[e]
        row = lax.broadcasted_iota(jnp.int32, (128, rows), 0)
        turned = jnp.where(row == 0, log_total, factor).T
        values = logits[cols, :]
        hit = target_mask(offset[0], targets, values.shape)
        soft = jnp.exp(values - turned[:, 0:1]) - jnp.where(hit, 1.0, 0.0)
        grad_out[cols, :] = (soft * turned[:, 1:2]).astype(bf16)
    loss_out[...] = jnp.broadcast_to(loss, loss_out.shape)


def row_grads(exits, offset, logits, own_stats, stats, targets, exit_scale):
    return call(
        functools.partial(grad_kernel, exits),
        "row_grads",
        [jax.ShapeDtypeStruct(logits.shape, bf16), jax.ShapeDtypeStruct((8, 128), f32)],
        [smem_spec] + [vmem_spec] * 4 + [smem_spec],
        [vmem_spec, vmem_spec],
    )(offset, logits, own_stats, stats, targets, exit_scale)


def block_kernel(n_tiles, has_added, ids, scaled, grads, *refs):
    added = refs[0] if has_added else None
    out, buf, sems = refs[-3:]
    tile = buf.shape[2]
    loads = []
    for t in range(n_tiles):
        source = scaled.at[ids[0], :, pl.ds(t * tile, tile)]
        loads.append(pltpu.make_async_copy(source, buf.at[t], sems.at[t]))
        loads[t].start()
    for t in range(n_tiles):
        loads[t].wait()
        total = lax.dot_general(
            buf[t], grads[...], (((0,), (0,)), ((), ())), preferred_element_type=f32
        )
        span = slice(t * tile, (t + 1) * tile)
        if has_added:
            total = total + added[span, :].astype(f32)
        out[span, :] = total.astype(out.dtype)


def grad_block(block, scaled, grads, added, dtype):
    _, rows, width = scaled.shape
    vocab = grads.shape[1]
    n_tiles = max(1, width // 512)
    tile = width // n_tiles
    args = [block, scaled, grads] + ([] if added is None else [added])
    specs = [smem_spec, hbm_spec, vmem_spec] + ([] if added is None else [vmem_spec])
    return call(
        functools.partial(block_kernel, n_tiles, added is not None),
        "grad_block",
        jax.ShapeDtypeStruct((width, vocab), dtype),
        specs,
        vmem_spec,
        scratch_shapes=[pltpu.VMEM((n_tiles, rows, tile), bf16), pltpu.SemaphoreType.DMA((n_tiles,))],
    )(*args)


def sum_kernel(a, b, *refs):
    refs[-1][...] = a[...] + b[...].astype(f32)


def sum_into(a, b, unit, units, whole):
    height, vocab = a.shape
    steps = max(1, height // 256)
    tile = height // steps
    spec = pl.BlockSpec((tile, vocab), lambda i: (i, 0))
    args = [a, b] + ([] if whole is None else [whole])
    return call(
        sum_kernel,
        "sum_into",
        jax.ShapeDtypeStruct((units * height, vocab), f32),
        [spec, spec] + ([] if whole is None else [hbm_spec]),
        pl.BlockSpec((tile, vocab), lambda i: (unit * steps + i, 0)),
        grid=(steps,),
        input_output_aliases={} if whole is None else {2: 0},
    )(*args)


def flip(axis, bit):
    return [(i, i ^ bit) for i in range(lax.axis_size(axis))]


def scalars(*values):
    return jnp.stack([v.astype(jnp.int32) for v in values])


def per_device(hidden_states, exit_layers, targets, norm_gain, exit_scale, unembedding):
    exits = exit_layers.shape[1]
    tokens = hidden_states.shape[1]
    full, vocab_local = unembedding.shape
    n_vocab, n_dp = lax.axis_size("vocab"), lax.axis_size("dp")
    ring_size = n_vocab // 2
    here = lax.axis_index("vocab")
    ring_at, side = here // 2, here % 2
    ring = [(j, (j + 2) % n_vocab) for j in range(n_vocab)]
    pair = flip("vocab", 1)
    layers = exit_layers.T
    gain = norm_gain.astype(f32).reshape(n_vocab, full // n_vocab)
    target_col = targets.reshape(tokens, 1)
    offset = scalars(here * vocab_local)

    states, scaled = [None] * exits, None
    current = [select(hidden_states, layers, e) for e in range(exits)]
    crossed, crossed_block = None, None
    for step in range(ring_size):
        owner = lax.rem(ring_at - step + ring_size, ring_size) * 2
        own_block, cross_block = owner + side, owner + 1 - side
        last = step == ring_size - 1
        crossing, coming = [], []
        for e in range(exits):
            piece = current[e]
            if crossed is not None:
                before = (e - 1) % exits
                piece, crossed[e], states[before] = bar((piece, crossed[e], states[before]))
            if last and step > 0 and e >= exits // 2:
                crossing.append(lax.ppermute(crossed[e], "vocab", ring))
            else:
                crossing.append(lax.ppermute(piece, "vocab", pair))
            if not last:
                coming.append(lax.ppermute(piece, "vocab", ring))
            pieces, ids = [piece], scalars(own_block)
            if crossed is not None:
                pieces, ids = [piece, crossed[e]], scalars(own_block, crossed_block)
            states[e], scaled = arrival(states[e], scaled, e, exits, ids, pieces, gain, unembedding)
        crossed, crossed_block, current = crossing, cross_block, coming
    logits, own_stats, scaled = last_blocks(
        states, scaled, scalars(*[crossed_block] * exits), offset, crossed, target_col, gain, unembedding
    )

    stats = own_stats
    bit = 1
    while bit < n_vocab:
        stats = merge(stats, lax.ppermute(stats, "vocab", flip("vocab", bit)))
        bit *= 2
    grads, loss = row_grads(exits, offset, logits, own_stats, stats, target_col, exit_scale)

    group = lax.axis_index("dp")
    high, low = group // 2, group % 2
    n_high = n_dp // 2
    units = n_vocab // n_dp

    def block_of(high_flip, low_index, unit):
        return scalars(((high ^ high_flip) * 2 + low_index) * units + unit)

    held = {}
    for high_flip in reversed(range(n_high)):
        came = []
        for unit in range(units):
            away = grad_block(block_of(high_flip, 1 - low, unit), scaled, grads, None, bf16)
            came.append(lax.ppermute(away, "dp", flip("dp", 1)))
        for unit in range(units):
            held[high_flip, unit] = grad_block(
                block_of(high_flip, low, unit), scaled, grads, came[unit], bf16 if high_flip else f32
            )
    loss, held[0, units - 1] = bar((loss, held[0, units - 1]))
    bit = 1
    while bit < n_dp:
        loss = loss + lax.ppermute(loss, "dp", flip("dp", bit))
        bit *= 2
    weight_grad = None
    bit = 1
    while bit < n_high:
        kept = {}
        for unit in range(units):
            for h in reversed(range(0, n_high, 2 * bit)):
                came = lax.ppermute(held[h + bit, unit], "dp", flip("dp", 2 * bit))
                if 2 * bit == n_high:
                    weight_grad = sum_into(held[h, unit], came, unit, units, weight_grad)
                else:
                    total = held[h, unit].astype(f32) + came.astype(f32)
                    kept[h, unit] = total.astype(bf16) if h else total
        held = kept
        bit *= 2
    mean_loss = loss[0, 0] / (tokens * n_dp)
    return (weight_grad, mean_loss)


def solution(mesh):
    in_specs = (P(None, "dp", "vocab"), P("dp", None), P("dp"), P(), P(), P(None, "vocab"))
    out_specs = (P("dp", "vocab"), P())
    return jax.shard_map(
        per_device, mesh=mesh, in_specs=in_specs, out_specs=out_specs, check_vma=False
    )
```

```python
import functools

import jax
import jax.numpy as jnp
from jax import lax
from jax.experimental import pallas as pl
from jax.experimental.pallas import tpu as pltpu
from jax.sharding import PartitionSpec as P

norm_eps = 1e-05
f32, bf16 = jnp.float32, jnp.bfloat16
vmem_bytes = 16 * 1024 * 1024
bar = lax.optimization_barrier
smem_spec = pl.BlockSpec(memory_space=pltpu.SMEM)
hbm_spec = pl.BlockSpec(memory_space=pltpu.HBM)
vmem_spec = pl.BlockSpec(memory_space=pltpu.VMEM)


def in_hbm(x):
    return pltpu.with_memory_space_constraint(x, pltpu.HBM)


def in_vmem(x):
    return pltpu.with_memory_space_constraint(x, pltpu.VMEM)


def call(kernel, name, out_shape, in_specs, out_specs, **more):
    return pl.pallas_call(
        kernel,
        name=name,
        out_shape=out_shape,
        in_specs=in_specs,
        out_specs=out_specs,
        compiler_params=pltpu.CompilerParams(vmem_limit_bytes=vmem_bytes),
        **more,
    )


def select_kernel(exit_index, row_len, layers_ref, hidden_ref, out_ref, sems):
    copies = []
    for r in range(layers_ref.shape[1]):
        span = pl.ds(r * row_len, row_len)
        source = hidden_ref.at[layers_ref[exit_index, r], span]
        copies.append(pltpu.make_async_copy(source, out_ref.at[span], sems.at[r]))
    for copy in copies:
        copy.start()
    for copy in copies:
        copy.wait()


def select(hidden, layers, exit_index):
    _, tokens, width = hidden.shape
    rows = layers.shape[1]
    return call(
        functools.partial(select_kernel, exit_index, tokens // rows),
        "select_rows",
        jax.ShapeDtypeStruct((tokens, width), hidden.dtype),
        [smem_spec, hbm_spec],
        pl.BlockSpec(memory_space=pl.ANY),
        scratch_shapes=[pltpu.SemaphoreType.DMA((rows,))],
    )(layers, in_hbm(hidden))


def block_index(place, ring_size, step, crossed):
    side = place[0] & 1
    owner = lax.rem((place[0] >> 1) + (ring_size - step), jnp.int32(ring_size))
    return owner * 2 + (1 - side if crossed else side)


def add_blocks(ids, pieces, spans, gain, unembedding, accs, sums, scaled_out):
    width = pieces[0].shape[1]
    lanes = min(128, width)
    for p in range(len(pieces)):
        x = pieces[p][...].astype(f32)
        scaled = (x * gain[pl.ds(ids[p], 1), :]).astype(bf16)
        scaled_out[ids[p], spans[p], :] = scaled
        weights = unembedding[pl.ds(pl.multiple_of(ids[p] * width, width), width), :]
        accs[p] = jnp.dot(scaled, weights, preferred_element_type=f32)
        square = x * x
        total = square[:, :lanes]
        for start in range(lanes, width, lanes):
            total = total + square[:, start : start + lanes]
        sums[p] = total


def arrival_kernel(n, first, makes, exit_index, ring_size, step, place, *refs):
    ids = [block_index(place, ring_size, step - p, p == 1) for p in range(n)]
    pieces, refs = refs[:n], refs[n:]
    gain, unembedding = refs[:2]
    refs = refs[2:]
    if not first:
        acc, ss = refs[:2]
        refs = refs[2:]
    if not makes:
        refs = refs[1:]
    acc_out, ss_out, scaled_out = refs
    rows = pieces[0].shape[0]
    span = pl.ds(exit_index * rows, rows)
    accs, sums = [None] * n, [None] * n
    add_blocks(ids, pieces, [span] * n, gain, unembedding, accs, sums, scaled_out)
    total, squares = accs[0], sums[0]
    for p in range(1, n):
        total, squares = total + accs[p], squares + sums[p]
    if not first:
        total, squares = total + acc[...], squares + ss[...]
    acc_out[...] = total
    ss_out[...] = squares


def arrival(state, scaled, exit_index, exits, ring_size, step, place, pieces, gain, unembedding):
    rows, width = pieces[0].shape
    full, vocab = unembedding.shape
    lanes = min(128, width)
    n = len(pieces)
    first, makes = state is None, scaled is None
    args = [place, *pieces, gain, in_vmem(unembedding)]
    specs = [smem_spec] + [vmem_spec] * (n + 2)
    aliases = {}
    if not first:
        aliases = {len(args): 0, len(args) + 1: 1}
        args += list(state)
        specs += [vmem_spec, vmem_spec]
    if not makes:
        aliases[len(args)] = 2
        args.append(in_vmem(scaled))
        specs.append(vmem_spec)
    acc, ss, scaled = call(
        functools.partial(arrival_kernel, n, first, makes, exit_index, ring_size, step),
        "arrival",
        [
            jax.ShapeDtypeStruct((rows, vocab), f32),
            jax.ShapeDtypeStruct((rows, lanes), f32),
            pltpu.VMEM((full // width, exits * rows, width), bf16),
        ],
        specs,
        [vmem_spec, vmem_spec, vmem_spec],
        input_output_aliases=aliases,
    )(*args)
    return (acc, ss), scaled


def target_mask(place, targets, shape):
    wanted = jnp.broadcast_to(targets[...].astype(f32), (128, shape[0])).T[:, 0:1]
    first = (place[0] * shape[1]).astype(f32)
    return lax.broadcasted_iota(jnp.int32, shape, 1).astype(f32) + first == wanted


def last_kernel(exits, full, ring_size, place, *refs):
    ids = [block_index(place, ring_size, ring_size - 1, True)] * exits
    pieces, refs = refs[:exits], refs[exits:]
    gain, unembedding = refs[:2]
    old_acc, old_ss, refs = refs[2 : 2 + exits], refs[2 + exits : 2 + 2 * exits], refs[2 + 2 * exits :]
    targets, _, logits_out, stats_out, scaled_out = refs
    rows = pieces[0].shape[0]
    spans = [pl.ds(e * rows, rows) for e in range(exits)]
    accs, sums = [None] * exits, [None] * exits
    add_blocks(ids, pieces, spans, gain, unembedding, accs, sums, scaled_out)
    for e in range(exits):
        square_sum = jnp.sum(old_ss[e][...] + sums[e], axis=1, keepdims=True)
        scale = lax.rsqrt(square_sum * (1.0 / full) + norm_eps)
        logits = (old_acc[e][...] + accs[e]) * scale
        logits_out[spans[e], :] = logits
        hit = target_mask(place, targets, logits.shape)
        target = jnp.sum(jnp.where(hit, logits, 0.0), axis=1, keepdims=True)
        top = jnp.max(logits, axis=1, keepdims=True)
        total = jnp.sum(jnp.exp(logits - top), axis=1, keepdims=True)
        lane = lax.broadcasted_iota(jnp.int32, (rows, 128), 1)
        packed = jnp.where(
            lane == 0, top, jnp.where(lane == 1, total, jnp.where(lane == 2, target, scale))
        )
        stats_out[:, e * rows : (e + 1) * rows] = packed.T[:8, :]


def last_blocks(states, scaled, ring_size, place, pieces, targets, gain, unembedding):
    exits = len(pieces)
    rows, width = pieces[0].shape
    full, vocab = unembedding.shape
    args = [place, *pieces, gain, in_vmem(unembedding)]
    args += [s[0] for s in states] + [s[1] for s in states] + [targets, in_vmem(scaled)]
    specs = [smem_spec] + [vmem_spec] * (3 * exits + 4)
    return call(
        functools.partial(last_kernel, exits, full, ring_size),
        "last_blocks",
        [
            jax.ShapeDtypeStruct((exits * rows, vocab), f32),
            jax.ShapeDtypeStruct((8, exits * rows), f32),
            pltpu.VMEM(scaled.shape, bf16),
        ],
        specs,
        [vmem_spec, vmem_spec, vmem_spec],
        input_output_aliases={len(args) - 1: 2},
    )(*args)


def merge_kernel(a, b, out):
    top_a, top_b = a[0:1, :], b[0:1, :]
    top = jnp.maximum(top_a, top_b)
    total = a[1:2, :] * jnp.exp(top_a - top) + b[1:2, :] * jnp.exp(top_b - top)
    target = a[2:3, :] + b[2:3, :]
    row = lax.broadcasted_iota(jnp.int32, out.shape, 0)
    out[...] = jnp.where(row == 0, top, jnp.where(row == 1, total, target))


def merge(a, b):
    shape = jax.ShapeDtypeStruct(a.shape, f32)
    return call(merge_kernel, "merge_stats", shape, [vmem_spec] * 2, vmem_spec)(a, b)


def grad_kernel(exits, place, logits, own_stats, stats, targets, exit_scale, grad_out, loss_out):
    rows = logits.shape[0] // exits
    loss = jnp.zeros((1, 1), f32)
    for e in range(exits):
        cols = slice(e * rows, (e + 1) * rows)
        log_total = stats[0:1, cols] + jnp.log(stats[1:2, cols])
        token_loss = log_total - stats[2:3, cols]
        loss = loss + exit_scale[e] * jnp.sum(token_loss, axis=1, keepdims=True)
        factor = own_stats[3:4, cols] * exit_scale[e]
        row = lax.broadcasted_iota(jnp.int32, (128, rows), 0)
        turned = jnp.where(row == 0, log_total, factor).T
        values = logits[cols, :]
        hit = target_mask(place, targets, values.shape)
        soft = jnp.exp(values - turned[:, 0:1]) - jnp.where(hit, 1.0, 0.0)
        grad_out[cols, :] = (soft * turned[:, 1:2]).astype(bf16)
    loss_out[...] = jnp.broadcast_to(loss, loss_out.shape)


def row_grads(exits, place, logits, own_stats, stats, targets, exit_scale):
    return call(
        functools.partial(grad_kernel, exits),
        "row_grads",
        [jax.ShapeDtypeStruct(logits.shape, bf16), jax.ShapeDtypeStruct((8, 128), f32)],
        [smem_spec] + [vmem_spec] * 4 + [smem_spec],
        [vmem_spec, vmem_spec],
    )(place, logits, own_stats, stats, targets, exit_scale)


def block_kernel(has_added, high_flip, away, units, unit, place, scaled, grads, *refs):
    out = refs[-1]
    low = place[1] & 1
    share = ((place[1] >> 1) ^ high_flip) * 2 + (1 - low if away else low)
    block = share * units + unit
    total = lax.dot_general(
        scaled[block], grads[...], (((0,), (0,)), ((), ())), preferred_element_type=f32
    )
    if has_added:
        total = total + refs[0][...].astype(f32)
    out[...] = total.astype(out.dtype)


def grad_block(high_flip, away, units, unit, place, scaled, grads, added, dtype):
    width, vocab = scaled.shape[2], grads.shape[1]
    args = [place, in_vmem(scaled), grads] + ([] if added is None else [added])
    return call(
        functools.partial(block_kernel, added is not None, high_flip, away, units, unit),
        "grad_block",
        jax.ShapeDtypeStruct((width, vocab), dtype),
        [smem_spec] + [vmem_spec] * (len(args) - 1),
        vmem_spec,
    )(*args)


def sum_kernel(a, b, *refs):
    refs[-1][...] = a[...] + b[...].astype(f32)


def sum_into(a, b, unit, units, whole):
    height, vocab = a.shape
    steps = max(1, height // 256)
    tile = height // steps
    spec = pl.BlockSpec((tile, vocab), lambda i: (i, 0))
    args = [a, b] + ([] if whole is None else [whole])
    return call(
        sum_kernel,
        "sum_into",
        jax.ShapeDtypeStruct((units * height, vocab), f32),
        [spec, spec] + ([] if whole is None else [hbm_spec]),
        pl.BlockSpec((tile, vocab), lambda i: (unit * steps + i, 0)),
        grid=(steps,),
        input_output_aliases={} if whole is None else {2: 0},
    )(*args)


def flip(axis, bit):
    return [(i, i ^ bit) for i in range(lax.axis_size(axis))]


def per_device(hidden_states, exit_layers, targets, norm_gain, exit_scale, unembedding):
    exits = exit_layers.shape[1]
    tokens = hidden_states.shape[1]
    full, vocab_local = unembedding.shape
    n_vocab, n_dp = lax.axis_size("vocab"), lax.axis_size("dp")
    ring_size = n_vocab // 2
    place = jnp.stack([lax.axis_index("vocab"), lax.axis_index("dp")]).astype(jnp.int32)
    ring = [(j, (j + 2) % n_vocab) for j in range(n_vocab)]
    pair = flip("vocab", 1)
    layers = exit_layers.T
    gain = norm_gain.astype(f32).reshape(n_vocab, full // n_vocab)
    target_row = targets.reshape(1, tokens)

    states, scaled = [None] * exits, None
    current = [select(hidden_states, layers, e) for e in range(exits)]
    crossed = None
    for step in range(ring_size):
        last = step == ring_size - 1
        crossing, coming = [], []
        for e in range(exits):
            piece = current[e]
            if crossed is not None:
                before = (e - 1) % exits
                piece, crossed[e], states[before] = bar((piece, crossed[e], states[before]))
            if last and step > 0 and e >= exits // 2:
                crossing.append(lax.ppermute(crossed[e], "vocab", ring))
            else:
                crossing.append(lax.ppermute(piece, "vocab", pair))
            if not last:
                coming.append(lax.ppermute(piece, "vocab", ring))
            pieces = [piece] if crossed is None else [piece, crossed[e]]
            states[e], scaled = arrival(
                states[e], scaled, e, exits, ring_size, step, place, pieces, gain, unembedding
            )
        crossed, current = crossing, coming
    logits, own_stats, scaled = last_blocks(
        states, scaled, ring_size, place, crossed, target_row, gain, unembedding
    )

    stats = own_stats
    bit = 1
    while bit < n_vocab:
        stats = merge(stats, lax.ppermute(stats, "vocab", flip("vocab", bit)))
        bit *= 2
    grads, loss = row_grads(exits, place, logits, own_stats, stats, target_row, exit_scale)

    n_high = n_dp // 2
    units = n_vocab // n_dp
    held = {}
    for high_flip in reversed(range(n_high)):
        came = []
        for unit in range(units):
            away = grad_block(high_flip, True, units, unit, place, scaled, grads, None, bf16)
            came.append(lax.ppermute(away, "dp", flip("dp", 1)))
        for unit in range(units):
            dtype = bf16 if high_flip else f32
            held[high_flip, unit] = grad_block(
                high_flip, False, units, unit, place, scaled, grads, came[unit], dtype
            )
    loss, held[0, units - 1] = bar((loss, held[0, units - 1]))
    bit = 1
    while bit < n_dp:
        loss = loss + lax.ppermute(loss, "dp", flip("dp", bit))
        bit *= 2
    weight_grad = None
    bit = 1
    while bit < n_high:
        kept = {}
        for unit in range(units):
            for h in reversed(range(0, n_high, 2 * bit)):
                came = lax.ppermute(held[h + bit, unit], "dp", flip("dp", 2 * bit))
                if 2 * bit == n_high:
                    weight_grad = sum_into(held[h, unit], came, unit, units, weight_grad)
                else:
                    total = held[h, unit].astype(f32) + came.astype(f32)
                    kept[h, unit] = total.astype(bf16) if h else total
        held = kept
        bit *= 2
    mean_loss = loss[0, 0] / (tokens * n_dp)
    return (weight_grad, mean_loss)


def solution(mesh):
    in_specs = (P(None, "dp", "vocab"), P("dp", None), P("dp"), P(), P(), P(None, "vocab"))
    out_specs = (P("dp", "vocab"), P())
    return jax.shard_map(
        per_device, mesh=mesh, in_specs=in_specs, out_specs=out_specs, check_vma=False
    )
```

```python
import functools

import jax
import jax.numpy as jnp
from jax import lax
from jax.experimental import pallas as pl
from jax.experimental.pallas import tpu as pltpu
from jax.sharding import PartitionSpec as P

norm_eps = 1e-05
f32, bf16 = jnp.float32, jnp.bfloat16
vmem_bytes = 16 * 1024 * 1024
bar = lax.optimization_barrier
smem_spec = pl.BlockSpec(memory_space=pltpu.SMEM)
hbm_spec = pl.BlockSpec(memory_space=pltpu.HBM)
vmem_spec = pl.BlockSpec(memory_space=pltpu.VMEM)


def in_hbm(x):
    return pltpu.with_memory_space_constraint(x, pltpu.HBM)


def in_vmem(x):
    return pltpu.with_memory_space_constraint(x, pltpu.VMEM)


def call(kernel, name, out_shape, in_specs, out_specs, **more):
    return pl.pallas_call(
        kernel,
        name=name,
        out_shape=out_shape,
        in_specs=in_specs,
        out_specs=out_specs,
        compiler_params=pltpu.CompilerParams(vmem_limit_bytes=vmem_bytes),
        **more,
    )


def select_kernel(exit_index, row_len, layers_ref, hidden_ref, out_ref, layers, layers_sem, sems):
    load = pltpu.make_async_copy(layers_ref, layers, layers_sem)
    load.start()
    load.wait()
    copies = []
    for r in range(layers.shape[1]):
        span = pl.ds(r * row_len, row_len)
        source = hidden_ref.at[layers[exit_index, r], span]
        copies.append(pltpu.make_async_copy(source, out_ref.at[span], sems.at[r]))
    for copy in copies:
        copy.start()
    for copy in copies:
        copy.wait()


def select(hidden, layers, exit_index):
    _, tokens, width = hidden.shape
    rows = layers.shape[1]
    return call(
        functools.partial(select_kernel, exit_index, tokens // rows),
        "select_rows",
        jax.ShapeDtypeStruct((tokens, width), hidden.dtype),
        [hbm_spec, hbm_spec],
        pl.BlockSpec(memory_space=pl.ANY),
        scratch_shapes=[
            pltpu.SMEM(layers.shape, jnp.int32),
            pltpu.SemaphoreType.DMA,
            pltpu.SemaphoreType.DMA((rows,)),
        ],
    )(in_hbm(layers), in_hbm(hidden))


def block_index(ring_size, step, crossed):
    here = lax.axis_index("vocab")
    side = here & 1
    owner = lax.rem((here >> 1) + (ring_size - step), jnp.int32(ring_size))
    return owner * 2 + (1 - side if crossed else side)


def add_blocks(ids, pieces, spans, gain, unembedding, accs, sums, scaled_out):
    width = pieces[0].shape[1]
    lanes = min(128, width)
    for p in range(len(pieces)):
        x = pieces[p][...].astype(f32)
        scaled = (x * gain[pl.ds(ids[p], 1), :]).astype(bf16)
        scaled_out[ids[p], :, spans[p]] = scaled.T
        weights = unembedding[pl.ds(pl.multiple_of(ids[p] * width, width), width), :]
        accs[p] = jnp.dot(scaled, weights, preferred_element_type=f32)
        square = x * x
        total = square[:, :lanes]
        for start in range(lanes, width, lanes):
            total = total + square[:, start : start + lanes]
        sums[p] = total


def arrival_kernel(n, first, makes, exit_index, ring_size, step, *refs):
    ids = [block_index(ring_size, step - p, p == 1) for p in range(n)]
    pieces, refs = refs[:n], refs[n:]
    gain, unembedding = refs[:2]
    refs = refs[2:]
    if not first:
        acc, ss = refs[:2]
        refs = refs[2:]
    if not makes:
        refs = refs[1:]
    acc_out, ss_out, scaled_out = refs
    rows = pieces[0].shape[0]
    span = pl.ds(exit_index * rows, rows)
    accs, sums = [None] * n, [None] * n
    add_blocks(ids, pieces, [span] * n, gain, unembedding, accs, sums, scaled_out)
    total, squares = accs[0], sums[0]
    for p in range(1, n):
        total, squares = total + accs[p], squares + sums[p]
    if not first:
        total, squares = total + acc[...], squares + ss[...]
    acc_out[...] = total
    ss_out[...] = squares


def arrival(state, scaled, exit_index, exits, ring_size, step, pieces, gain, unembedding):
    rows, width = pieces[0].shape
    full, vocab = unembedding.shape
    lanes = min(128, width)
    n = len(pieces)
    first, makes = state is None, scaled is None
    args = [*pieces, gain, in_vmem(unembedding)]
    specs = [vmem_spec] * (n + 2)
    aliases = {}
    if not first:
        aliases = {len(args): 0, len(args) + 1: 1}
        args += list(state)
        specs += [vmem_spec, vmem_spec]
    if not makes:
        aliases[len(args)] = 2
        args.append(in_vmem(scaled))
        specs.append(vmem_spec)
    acc, ss, scaled = call(
        functools.partial(arrival_kernel, n, first, makes, exit_index, ring_size, step),
        "arrival",
        [
            jax.ShapeDtypeStruct((rows, vocab), f32),
            jax.ShapeDtypeStruct((rows, lanes), f32),
            pltpu.VMEM((full // width, width, exits * rows), bf16),
        ],
        specs,
        [vmem_spec, vmem_spec, vmem_spec],
        input_output_aliases=aliases,
    )(*args)
    return (acc, ss), scaled


def target_mask(targets, shape):
    wanted = jnp.broadcast_to(targets[...].astype(f32), (128, shape[0])).T[:, 0:1]
    first = (lax.axis_index("vocab") * shape[1]).astype(f32)
    return lax.broadcasted_iota(jnp.int32, shape, 1).astype(f32) + first == wanted


def last_kernel(e, full, ring_size, piece, gain, unembedding, old_acc, old_ss, targets, *refs):
    logits_out, stats_out, scaled_out = refs[-3:]
    rows = piece.shape[0]
    span = pl.ds(e * rows, rows)
    accs, sums = [None], [None]
    ids = [block_index(ring_size, ring_size - 1, True)]
    add_blocks(ids, [piece], [span], gain, unembedding, accs, sums, scaled_out)
    square_sum = jnp.sum(old_ss[...] + sums[0], axis=1, keepdims=True)
    scale = lax.rsqrt(square_sum * (1.0 / full) + norm_eps)
    logits = (old_acc[...] + accs[0]) * scale
    logits_out[span, :] = logits
    hit = target_mask(targets, logits.shape)
    target = jnp.sum(jnp.where(hit, logits, 0.0), axis=1, keepdims=True)
    top = jnp.max(logits, axis=1, keepdims=True)
    total = jnp.sum(jnp.exp(logits - top), axis=1, keepdims=True)
    lane = lax.broadcasted_iota(jnp.int32, (rows, 128), 1)
    packed = jnp.where(
        lane == 0, top, jnp.where(lane == 1, total, jnp.where(lane == 2, target, scale))
    )
    stats_out[:, e * rows : (e + 1) * rows] = packed.T[:8, :]


def last_block(e, exits, state, scaled, outputs, ring_size, piece, targets, gain, unembedding):
    rows, width = piece.shape
    full, vocab = unembedding.shape
    args = [piece, gain, in_vmem(unembedding), *state, targets, *outputs, in_vmem(scaled)]
    n = len(args)
    aliases = {n - 1: 2}
    if outputs:
        aliases.update({n - 3: 0, n - 2: 1})
    *outputs, scaled = call(
        functools.partial(last_kernel, e, full, ring_size),
        "last_block",
        [
            jax.ShapeDtypeStruct((exits * rows, vocab), f32),
            jax.ShapeDtypeStruct((8, exits * rows), f32),
            pltpu.VMEM(scaled.shape, bf16),
        ],
        [vmem_spec] * n,
        [vmem_spec, vmem_spec, vmem_spec],
        input_output_aliases=aliases,
    )(*args)
    return outputs, scaled


def merge_kernel(a, b, out):
    top_a, top_b = a[0:1, :], b[0:1, :]
    top = jnp.maximum(top_a, top_b)
    total = a[1:2, :] * jnp.exp(top_a - top) + b[1:2, :] * jnp.exp(top_b - top)
    target = a[2:3, :] + b[2:3, :]
    row = lax.broadcasted_iota(jnp.int32, out.shape, 0)
    out[...] = jnp.where(row == 0, top, jnp.where(row == 1, total, target))


def merge(a, b):
    shape = jax.ShapeDtypeStruct(a.shape, f32)
    return call(merge_kernel, "merge_stats", shape, [vmem_spec] * 2, vmem_spec)(a, b)


def grad_kernel(exits, logits, own_stats, stats, targets, exit_scale, grad_out, loss_out):
    rows = logits.shape[0] // exits
    loss = jnp.zeros((1, 1), f32)
    for e in range(exits):
        cols = slice(e * rows, (e + 1) * rows)
        log_total = stats[0:1, cols] + jnp.log(stats[1:2, cols])
        token_loss = log_total - stats[2:3, cols]
        loss = loss + exit_scale[0:1, e : e + 1] * jnp.sum(token_loss, axis=1, keepdims=True)
        factor = own_stats[3:4, cols] * exit_scale[0:1, e : e + 1]
        row = lax.broadcasted_iota(jnp.int32, (128, rows), 0)
        turned = jnp.where(row == 0, log_total, factor).T
        values = logits[cols, :]
        hit = target_mask(targets, values.shape)
        soft = jnp.exp(values - turned[:, 0:1]) - jnp.where(hit, 1.0, 0.0)
        grad_out[cols, :] = (soft * turned[:, 1:2]).astype(bf16)
    loss_out[...] = jnp.broadcast_to(loss, loss_out.shape)


def row_grads(exits, logits, own_stats, stats, targets, exit_scale):
    return call(
        functools.partial(grad_kernel, exits),
        "row_grads",
        [jax.ShapeDtypeStruct(logits.shape, bf16), jax.ShapeDtypeStruct((8, 128), f32)],
        [vmem_spec] * 5,
        [vmem_spec, vmem_spec],
    )(logits, own_stats, stats, targets, exit_scale)


def block_kernel(has_added, high_flip, away, units, unit, scaled, grads, *refs):
    out = refs[-1]
    group = lax.axis_index("dp")
    low = group & 1
    share = ((group >> 1) ^ high_flip) * 2 + (1 - low if away else low)
    block = share * units + unit
    total = jnp.dot(scaled[block], grads[...], preferred_element_type=f32)
    if has_added:
        total = total + refs[0][...].astype(f32)
    out[...] = total.astype(out.dtype)


def grad_block(high_flip, away, units, unit, scaled, grads, added, dtype):
    width, vocab = scaled.shape[1], grads.shape[1]
    args = [in_vmem(scaled), grads] + ([] if added is None else [added])
    return call(
        functools.partial(block_kernel, added is not None, high_flip, away, units, unit),
        "grad_block",
        jax.ShapeDtypeStruct((width, vocab), dtype),
        [vmem_spec] * len(args),
        vmem_spec,
    )(*args)


def sum_kernel(units, tiles, n, count, *refs):
    parts, (loss, other, out, mean, buf, sems) = refs[: n * units], refs[n * units :]
    mean[...] = (loss[0:1, 0:1] + other[0:1, 0:1]) * (1.0 / count)
    height = parts[0].shape[0]
    tile = height // tiles
    copies = []
    for unit in range(units):
        for t in range(tiles):
            span = slice(t * tile, (t + 1) * tile)
            to = pl.ds(unit * height + t * tile, tile)
            total = parts[unit][span, :]
            for k in range(1, n):
                total = total + parts[k * units + unit][span, :].astype(f32)
            buf[to, :] = total
            copies.append(
                pltpu.make_async_copy(buf.at[to], out.at[to], sems.at[unit * tiles + t])
            )
            copies[-1].start()
    for copy in copies:
        copy.wait()


def sum_units(lists, loss, other, count):
    units = len(lists[0])
    height, vocab = lists[0][0].shape
    tiles = max(1, height // 256)
    return call(
        functools.partial(sum_kernel, units, tiles, len(lists), count),
        "sum_units",
        [
            jax.ShapeDtypeStruct((units * height, vocab), f32),
            jax.ShapeDtypeStruct((1, 1), f32),
        ],
        [vmem_spec] * (units * len(lists) + 2),
        [hbm_spec, vmem_spec],
        scratch_shapes=[
            pltpu.VMEM((units * height, vocab), f32),
            pltpu.SemaphoreType.DMA((units * tiles,)),
        ],
    )(*[part for parts in lists for part in parts], loss, other)


def flip(axis, bit):
    return [(i, i ^ bit) for i in range(lax.axis_size(axis))]


def per_device(hidden_states, exit_layers, targets, norm_gain, exit_scale, unembedding):
    exits = exit_layers.shape[1]
    tokens = hidden_states.shape[1]
    full, vocab_local = unembedding.shape
    n_vocab, n_dp = lax.axis_size("vocab"), lax.axis_size("dp")
    ring_size = n_vocab // 2
    ring = [(j, (j + 2) % n_vocab) for j in range(n_vocab)]
    pair = flip("vocab", 1)
    layers = exit_layers.T
    gain = norm_gain.astype(f32).reshape(n_vocab, full // n_vocab)
    target_row = targets.reshape(1, tokens)

    states, scaled = [None] * exits, None
    current = [select(hidden_states, layers, e) for e in range(exits)]
    crossed = None
    for step in range(ring_size):
        last = step == ring_size - 1
        crossing, coming = [], []
        for e in range(exits):
            piece = current[e]
            if crossed is not None:
                before = (e - 1) % exits
                piece, crossed[e], states[before] = bar((piece, crossed[e], states[before]))
            if not last:
                coming.append(lax.ppermute(piece, "vocab", ring))
            if last and step > 0 and e >= exits // 2:
                crossing.append(lax.ppermute(crossed[e], "vocab", ring))
            else:
                crossing.append(lax.ppermute(piece, "vocab", pair))
            pieces = [piece] if crossed is None else [piece, crossed[e]]
            states[e], scaled = arrival(
                states[e], scaled, e, exits, ring_size, step, pieces, gain, unembedding
            )
        crossed, current = crossing, coming
    outputs = ()
    for e in range(exits):
        outputs, scaled = last_block(
            e, exits, states[e], scaled, outputs, ring_size, crossed[e], target_row, gain, unembedding
        )
    logits, own_stats = outputs

    stats = own_stats
    bit = 1
    while bit < n_vocab:
        stats = merge(stats, lax.ppermute(stats, "vocab", flip("vocab", bit)))
        bit *= 2
    grads, loss = row_grads(exits, logits, own_stats, stats, target_row, exit_scale.reshape(1, exits))

    n_high = n_dp // 2
    units = n_vocab // n_dp
    held = {}
    for high_flip in reversed(range(n_high)):
        came = []
        for unit in range(units):
            away = grad_block(high_flip, True, units, unit, scaled, grads, None, bf16)
            came.append(lax.ppermute(away, "dp", flip("dp", 1)))
        for unit in range(units):
            held[high_flip, unit] = grad_block(
                high_flip, False, units, unit, scaled, grads,
                came[unit] if high_flip else None, bf16 if high_flip else f32,
            )
        if high_flip:
            grads, loss = bar((grads, loss, *[held[high_flip, unit] for unit in range(units)]))[:2]
    bit = 1
    while bit < n_high:
        loss = loss + lax.ppermute(loss, "dp", flip("dp", bit))
        bit *= 2
    other_loss = lax.ppermute(loss, "dp", flip("dp", bit))
    bit = 1
    while bit < n_high:
        kept = {}
        for h in reversed(range(0, n_high, 2 * bit)):
            over = [
                lax.ppermute(held[h + bit, unit], "dp", flip("dp", 2 * bit)) for unit in range(units)
            ]
            if 2 * bit == n_high:
                parts = [[held[0, unit] for unit in range(units)], came, over]
                weight_grad, mean_loss = sum_units(parts, loss, other_loss, tokens * n_dp)
            else:
                for unit in range(units):
                    total = held[h, unit].astype(f32) + over[unit].astype(f32)
                    kept[h, unit] = total.astype(bf16) if h else total
        held = kept
        bit *= 2
    return (weight_grad, mean_loss.reshape(()))


def solution(mesh):
    in_specs = (P(None, "dp", "vocab"), P("dp", None), P("dp"), P(), P(), P(None, "vocab"))
    out_specs = (P("dp", "vocab"), P())
    return jax.shard_map(
        per_device, mesh=mesh, in_specs=in_specs, out_specs=out_specs, check_vma=False
    )
```

```python
import functools

import jax
import jax.numpy as jnp
from jax import lax
from jax.experimental import pallas as pl
from jax.experimental.pallas import tpu as pltpu
from jax.sharding import PartitionSpec as P

norm_eps = 1e-05
f32, bf16 = jnp.float32, jnp.bfloat16
vmem_bytes = 16 * 1024 * 1024
bar = lax.optimization_barrier
smem_spec = pl.BlockSpec(memory_space=pltpu.SMEM)
hbm_spec = pl.BlockSpec(memory_space=pltpu.HBM)
vmem_spec = pl.BlockSpec(memory_space=pltpu.VMEM)


def in_hbm(x):
    return pltpu.with_memory_space_constraint(x, pltpu.HBM)


def in_vmem(x):
    return pltpu.with_memory_space_constraint(x, pltpu.VMEM)


def call(kernel, name, out_shape, in_specs, out_specs, **more):
    return pl.pallas_call(
        kernel,
        name=name,
        out_shape=out_shape,
        in_specs=in_specs,
        out_specs=out_specs,
        compiler_params=pltpu.CompilerParams(vmem_limit_bytes=vmem_bytes),
        **more,
    )


def select_kernel(exit_index, row_len, layers_ref, hidden_ref, out_ref, layers, layers_sem, sems):
    load = pltpu.make_async_copy(layers_ref, layers, layers_sem)
    load.start()
    load.wait()
    copies = []
    for r in range(layers.shape[1]):
        span = pl.ds(r * row_len, row_len)
        source = hidden_ref.at[layers[exit_index, r], span]
        copies.append(pltpu.make_async_copy(source, out_ref.at[span], sems.at[r]))
    for copy in copies:
        copy.start()
    for copy in copies:
        copy.wait()


def select(hidden, layers, exit_index):
    _, tokens, width = hidden.shape
    rows = layers.shape[1]
    return call(
        functools.partial(select_kernel, exit_index, tokens // rows),
        "select_rows",
        jax.ShapeDtypeStruct((tokens, width), hidden.dtype),
        [hbm_spec, hbm_spec],
        pl.BlockSpec(memory_space=pl.ANY),
        scratch_shapes=[
            pltpu.SMEM(layers.shape, jnp.int32),
            pltpu.SemaphoreType.DMA,
            pltpu.SemaphoreType.DMA((rows,)),
        ],
    )(in_hbm(layers), in_hbm(hidden))


def owner_index(ring_size, step):
    return lax.rem((lax.axis_index("vocab") >> 1) + (ring_size - step), jnp.int32(ring_size))


def block_index(ring_size, step, crossed):
    side = lax.axis_index("vocab") & 1
    return owner_index(ring_size, step) * 2 + (1 - side if crossed else side)


def add_blocks(ids, pieces, spans, gain, unembedding, accs, sums, scaled_out):
    width = pieces[0].shape[1]
    lanes = min(128, width)
    for p in range(len(pieces)):
        x = pieces[p][...].astype(f32)
        scaled = (x * gain[pl.ds(ids[p], 1), :]).astype(bf16)
        scaled_out[ids[p], :, spans[p]] = scaled.T
        weights = unembedding[pl.ds(pl.multiple_of(ids[p] * width, width), width), :]
        accs[p] = jnp.dot(scaled, weights, preferred_element_type=f32)
        square = x * x
        total = square[:, :lanes]
        for start in range(lanes, width, lanes):
            total = total + square[:, start : start + lanes]
        sums[p] = total


def arrival_kernel(n, first, makes, exit_index, ring_size, step, *refs):
    ids = [block_index(ring_size, step - p, p == 1) for p in range(n)]
    pieces, refs = refs[:n], refs[n:]
    gain, unembedding = refs[:2]
    refs = refs[2:]
    if not first:
        acc, ss = refs[:2]
        refs = refs[2:]
    if not makes:
        refs = refs[1:]
    acc_out, ss_out, scaled_out = refs
    rows = pieces[0].shape[0]
    span = pl.ds(exit_index * rows, rows)
    accs, sums = [None] * n, [None] * n
    add_blocks(ids, pieces, [span] * n, gain, unembedding, accs, sums, scaled_out)
    total, squares = accs[0], sums[0]
    for p in range(1, n):
        total, squares = total + accs[p], squares + sums[p]
    if not first:
        total, squares = total + acc[...], squares + ss[...]
    acc_out[...] = total
    ss_out[...] = squares


def arrival(state, scaled, exit_index, exits, ring_size, step, pieces, gain, unembedding):
    rows, width = pieces[0].shape
    full, vocab = unembedding.shape
    lanes = min(128, width)
    n = len(pieces)
    first, makes = state is None, scaled is None
    args = [*pieces, gain, in_vmem(unembedding)]
    specs = [vmem_spec] * (n + 2)
    aliases = {}
    if not first:
        aliases = {len(args): 0, len(args) + 1: 1}
        args += list(state)
        specs += [vmem_spec, vmem_spec]
    if not makes:
        aliases[len(args)] = 2
        args.append(in_vmem(scaled))
        specs.append(vmem_spec)
    acc, ss, scaled = call(
        functools.partial(arrival_kernel, n, first, makes, exit_index, ring_size, step),
        "arrival",
        [
            jax.ShapeDtypeStruct((rows, vocab), f32),
            jax.ShapeDtypeStruct((rows, lanes), f32),
            pltpu.VMEM((full // width, width, exits * rows), bf16),
        ],
        specs,
        [vmem_spec, vmem_spec, vmem_spec],
        input_output_aliases=aliases,
    )(*args)
    return (acc, ss), scaled


def pull_kernel(ring_size, step, e, *refs):
    piece, gain, (own_out, relay_out) = refs[0], refs[1], refs[-2:]
    rows = piece.shape[0]
    owner, group = owner_index(ring_size, step), lax.axis_index("dp")

    @pl.when((owner >> 1) == (group >> 1))
    def _():
        block = owner * 2 + (lax.axis_index("vocab") & 1)
        x = piece[...].astype(f32) * gain[pl.ds(block, 1), :]
        turned = x.astype(bf16).T

        @pl.when(owner == group)
        def _():
            own_out[:, e * rows : (e + 1) * rows] = turned

        @pl.when(owner != group)
        def _():
            relay_out[:, e * rows : (e + 1) * rows] = turned


def pull(pulled, e, exits, ring_size, step, piece, gain):
    rows, width = piece.shape
    args = [piece, gain] + ([] if pulled is None else [in_vmem(x) for x in pulled])
    return call(
        functools.partial(pull_kernel, ring_size, step, e),
        "pull",
        [pltpu.VMEM((width, exits * rows), bf16)] * 2,
        [vmem_spec] * len(args),
        [vmem_spec] * 2,
        input_output_aliases={} if pulled is None else {2: 0, 3: 1},
    )(*args)


def target_mask(wanted, shape):
    first = (lax.axis_index("vocab") * shape[1]).astype(f32)
    return lax.broadcasted_iota(jnp.int32, shape, 1).astype(f32) + first == wanted


def last_kernel(e, full, ring_size, piece, gain, unembedding, old_acc, old_ss, targets, *refs):
    logits_out, stats_out, scaled_out = refs[-3:]
    rows = piece.shape[0]
    span = pl.ds(e * rows, rows)
    accs, sums = [None], [None]
    ids = [block_index(ring_size, ring_size - 1, True)]
    add_blocks(ids, [piece], [span], gain, unembedding, accs, sums, scaled_out)
    square_sum = jnp.sum(old_ss[...] + sums[0], axis=1, keepdims=True)
    scale = lax.rsqrt(square_sum * (1.0 / full) + norm_eps)
    logits = (old_acc[...] + accs[0]) * scale
    logits_out[...] = logits
    wanted = jnp.broadcast_to(targets[...].astype(f32), (128, rows)).T[:, 0:1]
    hit = target_mask(wanted, logits.shape)
    target = jnp.sum(jnp.where(hit, logits, 0.0), axis=1, keepdims=True)
    top = jnp.max(logits, axis=1, keepdims=True)
    total = jnp.sum(jnp.exp(logits - top), axis=1, keepdims=True)
    lane = lax.broadcasted_iota(jnp.int32, (rows, 128), 1)
    packed = jnp.where(
        lane == 0, top, jnp.where(lane == 1, total, jnp.where(lane == 2, target, scale))
    )
    packed = jnp.where(lane == 4, wanted, packed)
    stats_out[...] = packed.T[:8, :]


def last_block(e, exits, state, scaled, ring_size, piece, targets, gain, unembedding):
    rows, width = piece.shape
    full, vocab = unembedding.shape
    args = [piece, gain, in_vmem(unembedding), *state, targets, in_vmem(scaled)]
    n = len(args)
    return call(
        functools.partial(last_kernel, e, full, ring_size),
        "last_block",
        [
            jax.ShapeDtypeStruct((rows, vocab), f32),
            jax.ShapeDtypeStruct((8, rows), f32),
            pltpu.VMEM(scaled.shape, bf16),
        ],
        [vmem_spec] * n,
        [vmem_spec, vmem_spec, vmem_spec],
        input_output_aliases={n - 1: 2},
    )(*args)


def merge_kernel(n, *refs):
    out = refs[-1]
    rows = refs[0].shape[1]
    for k in range(n):
        a, b = refs[2 * k], refs[2 * k + 1]
        top_a, top_b = a[0:1, :], b[0:1, :]
        top = jnp.maximum(top_a, top_b)
        total = a[1:2, :] * jnp.exp(top_a - top) + b[1:2, :] * jnp.exp(top_b - top)
        target = a[2:3, :] + b[2:3, :]
        row = lax.broadcasted_iota(jnp.int32, (out.shape[0], rows), 0)
        merged = jnp.where(row == 0, top, jnp.where(row == 1, total, target))
        merged = jnp.where(row > 2, a[...], merged)
        out[:, k * rows : (k + 1) * rows] = merged


def merge(*pairs):
    rows = pairs[0][0].shape[1]
    shape = jax.ShapeDtypeStruct((8, len(pairs) * rows), f32)
    kernel = functools.partial(merge_kernel, len(pairs))
    args = [x for pair in pairs for x in pair]
    return call(kernel, "merge_stats", shape, [vmem_spec] * len(args), vmem_spec)(*args)


def exit_grads(e, values, stats, exit_scale):
    rows = values.shape[0]
    cols = slice(e * rows, (e + 1) * rows)
    weight = exit_scale[0:1, e : e + 1]
    log_total = stats[0:1, cols] + jnp.log(stats[1:2, cols])
    loss = weight * jnp.sum(log_total - stats[2:3, cols], axis=1, keepdims=True)
    factor = stats[3:4, cols] * weight
    row = lax.broadcasted_iota(jnp.int32, (128, rows), 0)
    turned = jnp.where(row == 0, log_total, jnp.where(row == 1, factor, stats[4:5, cols])).T
    hit = target_mask(turned[:, 2:3], values.shape)
    soft = jnp.exp(values - turned[:, 0:1]) - jnp.where(hit, 1.0, 0.0)
    return (soft * turned[:, 1:2]).astype(bf16), loss


def grad_kernel(exits, *refs):
    logits, (stats, exit_scale, grad_out, loss_out) = refs[:exits], refs[exits:]
    rows = logits[0].shape[0]
    total = jnp.zeros((1, 1), f32)
    for e in range(exits):
        grads, loss = exit_grads(e, logits[e][...], stats, exit_scale)
        grad_out[e * rows : (e + 1) * rows, :] = grads
        total = total + loss
    loss_out[...] = jnp.broadcast_to(total, loss_out.shape)


def row_grads(logits, stats, exit_scale):
    exits = len(logits)
    rows, vocab = logits[0].shape
    return call(
        functools.partial(grad_kernel, exits),
        "row_grads",
        [jax.ShapeDtypeStruct((exits * rows, vocab), bf16), jax.ShapeDtypeStruct((8, 128), f32)],
        [vmem_spec] * (exits + 2),
        [vmem_spec, vmem_spec],
    )(*logits, stats, exit_scale)


def block_kernel(has_added, high_flip, away, units, unit, scaled, grads, *refs):
    out = refs[-1]
    group = lax.axis_index("dp")
    low = group & 1
    share = ((group >> 1) ^ high_flip) * 2 + (1 - low if away else low)
    if unit == "crossed":
        unit = 1 - (lax.axis_index("vocab") & 1)
    elif unit == "own":
        unit = lax.axis_index("vocab") & 1
    block = share * units + unit
    total = jnp.dot(scaled[block], grads[...], preferred_element_type=f32)
    if has_added:
        total = total + refs[0][...].astype(f32)
    out[...] = total.astype(out.dtype)


def grad_block(high_flip, away, units, unit, scaled, grads, added, dtype):
    width, vocab = scaled.shape[1], grads.shape[1]
    args = [in_vmem(scaled), grads] + ([] if added is None else [added])
    return call(
        functools.partial(block_kernel, added is not None, high_flip, away, units, unit),
        "grad_block",
        jax.ShapeDtypeStruct((width, vocab), dtype),
        [vmem_spec] * len(args),
        vmem_spec,
    )(*args)


def sum_kernel(units, tiles, n, count, *refs):
    parts, (loss, other, out, mean, buf, sems) = refs[: n * units], refs[n * units :]
    mean[...] = (loss[0:1, 0:1] + other[0:1, 0:1]) * (1.0 / count)
    height = parts[0].shape[0]
    tile = height // tiles
    copies = []
    for unit in range(units):
        for t in range(tiles):
            span = slice(t * tile, (t + 1) * tile)
            to = pl.ds(unit * height + t * tile, tile)
            total = parts[unit][span, :]
            for k in range(1, n):
                total = total + parts[k * units + unit][span, :].astype(f32)
            buf[to, :] = total
            copies.append(
                pltpu.make_async_copy(buf.at[to], out.at[to], sems.at[unit * tiles + t])
            )
            copies[-1].start()
    for copy in copies:
        copy.wait()


def sum_units(lists, loss, other, count):
    units = len(lists[0])
    height, vocab = lists[0][0].shape
    tiles = max(1, height // 256)
    return call(
        functools.partial(sum_kernel, units, tiles, len(lists), count),
        "sum_units",
        [
            jax.ShapeDtypeStruct((units * height, vocab), f32),
            jax.ShapeDtypeStruct((1, 1), f32),
        ],
        [vmem_spec] * (units * len(lists) + 2),
        [hbm_spec, vmem_spec],
        scratch_shapes=[
            pltpu.VMEM((units * height, vocab), f32),
            pltpu.SemaphoreType.DMA((units * tiles,)),
        ],
    )(*[part for parts in lists for part in parts], loss, other)


def own_kernel(exits, count, *refs):
    logits, refs = refs[: 2 * exits], refs[2 * exits :]
    stats, refs = refs[:2], refs[2:]
    exit_scale, *pulled, scaled, grads, came_own, came_crossed, loss, loss_core = refs[:9]
    out, part, mean, buf, sem = refs[9:]
    rows = logits[0].shape[0]
    height = buf.shape[0]
    side = lax.axis_index("vocab") & 1
    block = lax.axis_index("dp") * 2
    total = jnp.dot(scaled[block + side], grads[...], preferred_element_type=f32)
    total = total + came_own[...].astype(f32)
    total_loss = loss[0:1, 0:1] + loss_core[0:1, 0:1]
    for k in range(2):
        for e in range(exits):
            values = logits[k * exits + e][...]
            other, loss_part = exit_grads(e, values, stats[k], exit_scale)
            total_loss = total_loss + loss_part
            rows_of = pulled[k][:, e * rows : (e + 1) * rows]
            total = total + jnp.dot(rows_of, other, preferred_element_type=f32)
    buf[...] = total
    to = pl.ds(pl.multiple_of(side * height, height), height)
    copy = pltpu.make_async_copy(buf, out.at[to], sem)
    copy.start()
    mean[...] = total_loss * (1.0 / count)
    crossed = jnp.dot(scaled[block + 1 - side], grads[...], preferred_element_type=f32)
    part[...] = crossed + came_crossed[...].astype(f32)
    copy.wait()


def own_block(logits, stats, exit_scale, pulled, scaled, grads, came, losses, count):
    exits = exit_scale.shape[1]
    height, vocab = came[0].shape
    args = [*logits, *stats, exit_scale, *pulled, in_vmem(scaled), grads, *came, *losses]
    return call(
        functools.partial(own_kernel, exits, count),
        "own_block",
        [
            jax.ShapeDtypeStruct((2 * height, vocab), f32),
            jax.ShapeDtypeStruct((height, vocab), f32),
            jax.ShapeDtypeStruct((1, 1), f32),
        ],
        [vmem_spec] * len(args),
        [hbm_spec, vmem_spec, vmem_spec],
        scratch_shapes=[pltpu.VMEM((height, vocab), f32), pltpu.SemaphoreType.DMA],
    )(*args)


def crossed_kernel(tiles, part, over, _, out, buf, sems):
    height = part.shape[0]
    tile = height // tiles
    start = (1 - (lax.axis_index("vocab") & 1)) * height
    copies = []
    for t in range(tiles):
        span = slice(t * tile, (t + 1) * tile)
        buf[span, :] = part[span, :] + over[span, :].astype(f32)
        to = pl.ds(pl.multiple_of(start + t * tile, tile), tile)
        copies.append(pltpu.make_async_copy(buf.at[pl.ds(t * tile, tile)], out.at[to], sems.at[t]))
        copies[t].start()
    for copy in copies:
        copy.wait()


def crossed_block(part, over, out):
    height, vocab = part.shape
    tiles = max(1, height // 256)
    return call(
        functools.partial(crossed_kernel, tiles),
        "crossed_block",
        jax.ShapeDtypeStruct(out.shape, f32),
        [vmem_spec, vmem_spec, hbm_spec],
        hbm_spec,
        input_output_aliases={2: 0},
        scratch_shapes=[pltpu.VMEM((height, vocab), f32), pltpu.SemaphoreType.DMA((tiles,))],
    )(part, over, out)


def flip(axis, bit):
    return [(i, i ^ bit) for i in range(lax.axis_size(axis))]


def per_device(hidden_states, exit_layers, targets, norm_gain, exit_scale, unembedding):
    exits = exit_layers.shape[1]
    tokens = hidden_states.shape[1]
    full, vocab_local = unembedding.shape
    n_vocab, n_dp = lax.axis_size("vocab"), lax.axis_size("dp")
    ring_size = n_vocab // 2
    ring = [(j, (j + 2) % n_vocab) for j in range(n_vocab)]
    pair = flip("vocab", 1)
    layers = exit_layers.T
    gain = norm_gain.astype(f32).reshape(n_vocab, full // n_vocab)
    target_row = targets.reshape(1, tokens)

    paired = n_dp == 4 and n_vocab == 2 * n_dp

    def pull_pairs(step):
        pairs = []
        for d in range(n_dp):
            for j in range(n_vocab):
                if (j // 2 - step) % ring_size // 2 != d // 2:
                    pairs.append((d * n_vocab + j, (d ^ 2) * n_vocab + j))
        return pairs

    states, scaled = [None] * exits, None
    current = [select(hidden_states, layers, e) for e in range(exits)]
    crossed, pulled, pending = None, None, None
    for step in range(ring_size):
        last = step == ring_size - 1
        crossing, coming = [], []
        for e in range(exits):
            piece = current[e]
            if crossed is not None:
                before = (e - 1) % exits
                piece, crossed[e], states[before] = bar((piece, crossed[e], states[before]))
            elif e:
                piece, states[e - 1] = bar((piece, states[e - 1]))
            if not last:
                coming.append(lax.ppermute(piece, "vocab", ring))
            if last and step > 0 and e >= exits // 2:
                crossing.append(lax.ppermute(crossed[e], "vocab", ring))
            else:
                crossing.append(lax.ppermute(piece, "vocab", pair))
            sent = lax.ppermute(piece, ("dp", "vocab"), pull_pairs(step)) if paired else None
            if pending is not None:
                piece, came = bar((piece, pending[2]))
                pulled = pull(pulled, pending[1], exits, ring_size, pending[0], came, gain)
            pending = (step, e, sent) if paired else None
            pieces = [piece] if crossed is None else [piece, crossed[e]]
            states[e], scaled = arrival(
                states[e], scaled, e, exits, ring_size, step, pieces, gain, unembedding
            )
        crossed, current = crossing, coming

    def over_y(x):
        return lax.ppermute(x, "dp", flip("dp", 2))

    def over_core(x):
        return lax.ppermute(x, "dp", flip("dp", 1))

    logits, own_stats, partner_stats = [], [], []
    for e in range(exits):
        if e:
            crossed[e], partner_stats[e - 1] = bar((crossed[e], partner_stats[e - 1]))
        values, stats, scaled = last_block(
            e, exits, states[e], scaled, ring_size, crossed[e], target_row, gain, unembedding
        )
        logits.append(values)
        own_stats.append(stats)
        partner_stats.append(lax.ppermute(stats, "vocab", pair))
    stats = merge(*zip(own_stats, partner_stats))
    scale_row = exit_scale.reshape(1, exits)
    if paired:
        y_logits = [over_y(values) for values in logits]
    bit = 2
    while bit < n_vocab:
        if 2 * bit == n_vocab and paired:
            stats, came = bar((stats, pending[2]))
        stats = merge((stats, lax.ppermute(stats, "vocab", flip("vocab", bit))))
        bit *= 2
    if paired:
        pulled = pull(pulled, pending[1], exits, ring_size, pending[0], came, gain)
        y_stats = over_y(stats)
        y_logits, pulled = bar((y_logits, pulled, stats))[:2]
        yc_logits = [over_core(values) for values in y_logits]
        pulled = (pulled[0], over_core(pulled[1]))
    grads, loss = row_grads(logits, stats, scale_row)

    if paired:
        away = grad_block(1, True, 2, "crossed", scaled, grads, None, bf16)
        came, y_stats = bar((over_core(away), y_stats))
        home = grad_block(1, False, 2, "crossed", scaled, grads, came, bf16)
        over = over_y(home)
        grads, loss = bar((grads, loss, home))[:2]
        came = []
        for unit in ("own", "crossed"):
            came.append(over_core(grad_block(0, True, 2, unit, scaled, grads, None, bf16)))
        weight_grad, part, mean_loss = own_block(
            y_logits + yc_logits, (y_stats, over_core(y_stats)), scale_row,
            pulled, scaled, grads, came, (loss, over_core(loss)), tokens * n_dp,
        )
        return (crossed_block(part, over, weight_grad), mean_loss.reshape(()))

    n_high = n_dp // 2
    units = n_vocab // n_dp
    held = {}
    for high_flip in reversed(range(n_high)):
        came = []
        for unit in range(units):
            away = grad_block(high_flip, True, units, unit, scaled, grads, None, bf16)
            came.append(lax.ppermute(away, "dp", flip("dp", 1)))
        for unit in range(units):
            held[high_flip, unit] = grad_block(
                high_flip, False, units, unit, scaled, grads,
                came[unit] if high_flip else None, bf16 if high_flip else f32,
            )
        if high_flip:
            grads, loss = bar((grads, loss, *[held[high_flip, unit] for unit in range(units)]))[:2]
    bit = 1
    while bit < n_high:
        loss = loss + lax.ppermute(loss, "dp", flip("dp", bit))
        bit *= 2
    other_loss = lax.ppermute(loss, "dp", flip("dp", bit))
    bit = 1
    while bit < n_high:
        kept = {}
        for h in reversed(range(0, n_high, 2 * bit)):
            over = [
                lax.ppermute(held[h + bit, unit], "dp", flip("dp", 2 * bit)) for unit in range(units)
            ]
            if 2 * bit == n_high:
                parts = [[held[0, unit] for unit in range(units)], came, over]
                weight_grad, mean_loss = sum_units(parts, loss, other_loss, tokens * n_dp)
            else:
                for unit in range(units):
                    total = held[h, unit].astype(f32) + over[unit].astype(f32)
                    kept[h, unit] = total.astype(bf16) if h else total
        held = kept
        bit *= 2
    return (weight_grad, mean_loss.reshape(()))


def solution(mesh):
    in_specs = (P(None, "dp", "vocab"), P("dp", None), P("dp"), P(), P(), P(None, "vocab"))
    out_specs = (P("dp", "vocab"), P())
    return jax.shard_map(
        per_device, mesh=mesh, in_specs=in_specs, out_specs=out_specs, check_vma=False
    )
```

```python
import functools

import jax
import jax.numpy as jnp
from jax import lax
from jax.experimental import pallas as pl
from jax.experimental.pallas import tpu as pltpu
from jax.sharding import PartitionSpec as P

norm_eps = 1e-05
f32, bf16 = jnp.float32, jnp.bfloat16
vmem_bytes = 16 * 1024 * 1024
bar = lax.optimization_barrier
smem_spec = pl.BlockSpec(memory_space=pltpu.SMEM)
hbm_spec = pl.BlockSpec(memory_space=pltpu.HBM)
vmem_spec = pl.BlockSpec(memory_space=pltpu.VMEM)


def in_hbm(x):
    return pltpu.with_memory_space_constraint(x, pltpu.HBM)


def in_vmem(x):
    return pltpu.with_memory_space_constraint(x, pltpu.VMEM)


def call(kernel, name, out_shape, in_specs, out_specs, **more):
    return pl.pallas_call(
        kernel,
        name=name,
        out_shape=out_shape,
        in_specs=in_specs,
        out_specs=out_specs,
        compiler_params=pltpu.CompilerParams(vmem_limit_bytes=vmem_bytes),
        **more,
    )


def select_kernel(exit_index, row_len, layers_ref, hidden_ref, out_ref, layers, layers_sem, sems):
    load = pltpu.make_async_copy(layers_ref, layers, layers_sem)
    load.start()
    load.wait()
    copies = []
    for r in range(layers.shape[1]):
        span = pl.ds(r * row_len, row_len)
        source = hidden_ref.at[layers[exit_index, r], span]
        copies.append(pltpu.make_async_copy(source, out_ref.at[span], sems.at[r]))
    for copy in copies:
        copy.start()
    for copy in copies:
        copy.wait()


def select(hidden, layers, exit_index):
    _, tokens, width = hidden.shape
    rows = layers.shape[1]
    return call(
        functools.partial(select_kernel, exit_index, tokens // rows),
        "select_rows",
        jax.ShapeDtypeStruct((tokens, width), hidden.dtype),
        [hbm_spec, hbm_spec],
        pl.BlockSpec(memory_space=pl.ANY),
        scratch_shapes=[
            pltpu.SMEM(layers.shape, jnp.int32),
            pltpu.SemaphoreType.DMA,
            pltpu.SemaphoreType.DMA((rows,)),
        ],
    )(in_hbm(layers), in_hbm(hidden))


def owner_index(ring_size, step):
    return lax.rem((lax.axis_index("vocab") >> 1) + (ring_size - step), jnp.int32(ring_size))


def block_index(ring_size, step, crossed):
    side = lax.axis_index("vocab") & 1
    return owner_index(ring_size, step) * 2 + (1 - side if crossed else side)


def add_blocks(ids, pieces, spans, gain, unembedding, accs, sums, scaled_out):
    width = pieces[0].shape[1]
    lanes = min(128, width)
    for p in range(len(pieces)):
        x = pieces[p][...].astype(f32)
        scaled = (x * gain[pl.ds(ids[p], 1), :]).astype(bf16)
        scaled_out[ids[p], :, spans[p]] = scaled.T
        weights = unembedding[pl.ds(pl.multiple_of(ids[p] * width, width), width), :]
        accs[p] = jnp.dot(scaled, weights, preferred_element_type=f32)
        square = x * x
        total = square[:, :lanes]
        for start in range(lanes, width, lanes):
            total = total + square[:, start : start + lanes]
        sums[p] = total


def arrival_kernel(n, first, makes, exit_index, ring_size, step, *refs):
    ids = [block_index(ring_size, step - p, p == 1) for p in range(n)]
    pieces, refs = refs[:n], refs[n:]
    gain, unembedding = refs[:2]
    refs = refs[2:]
    if not first:
        acc, ss = refs[:2]
        refs = refs[2:]
    if not makes:
        refs = refs[1:]
    acc_out, ss_out, scaled_out = refs
    rows = pieces[0].shape[0]
    span = pl.ds(exit_index * rows, rows)
    accs, sums = [None] * n, [None] * n
    add_blocks(ids, pieces, [span] * n, gain, unembedding, accs, sums, scaled_out)
    total, squares = accs[0], sums[0]
    for p in range(1, n):
        total, squares = total + accs[p], squares + sums[p]
    if not first:
        total, squares = total + acc[...], squares + ss[...]
    acc_out[...] = total
    ss_out[...] = squares


def arrival(state, scaled, exit_index, exits, ring_size, step, pieces, gain, unembedding):
    rows, width = pieces[0].shape
    full, vocab = unembedding.shape
    lanes = min(128, width)
    n = len(pieces)
    first, makes = state is None, scaled is None
    args = [*pieces, gain, in_vmem(unembedding)]
    specs = [vmem_spec] * (n + 2)
    aliases = {}
    if not first:
        aliases = {len(args): 0, len(args) + 1: 1}
        args += list(state)
        specs += [vmem_spec, vmem_spec]
    if not makes:
        aliases[len(args)] = 2
        args.append(in_vmem(scaled))
        specs.append(vmem_spec)
    acc, ss, scaled = call(
        functools.partial(arrival_kernel, n, first, makes, exit_index, ring_size, step),
        "arrival",
        [
            jax.ShapeDtypeStruct((rows, vocab), f32),
            jax.ShapeDtypeStruct((rows, lanes), f32),
            pltpu.VMEM((full // width, width, exits * rows), bf16),
        ],
        specs,
        [vmem_spec, vmem_spec, vmem_spec],
        input_output_aliases=aliases,
    )(*args)
    return (acc, ss), scaled


def pull_kernel(ring_size, step, e, *refs):
    piece, gain, (own_out, relay_out) = refs[0], refs[1], refs[-2:]
    rows = piece.shape[0]
    owner, group = owner_index(ring_size, step), lax.axis_index("dp")

    @pl.when((owner >> 1) == (group >> 1))
    def _():
        block = owner * 2 + (lax.axis_index("vocab") & 1)
        x = piece[...].astype(f32) * gain[pl.ds(block, 1), :]
        turned = x.astype(bf16).T

        @pl.when(owner == group)
        def _():
            own_out[:, e * rows : (e + 1) * rows] = turned

        @pl.when(owner != group)
        def _():
            relay_out[:, e * rows : (e + 1) * rows] = turned


def pull(pulled, e, exits, ring_size, step, piece, gain):
    rows, width = piece.shape
    args = [piece, gain] + ([] if pulled is None else [in_vmem(x) for x in pulled])
    return call(
        functools.partial(pull_kernel, ring_size, step, e),
        "pull",
        [pltpu.VMEM((width, exits * rows), bf16)] * 2,
        [vmem_spec] * len(args),
        [vmem_spec] * 2,
        input_output_aliases={} if pulled is None else {2: 0, 3: 1},
    )(*args)


def target_mask(wanted, shape):
    first = (lax.axis_index("vocab") * shape[1]).astype(f32)
    return lax.broadcasted_iota(jnp.int32, shape, 1).astype(f32) + first == wanted


def last_kernel(e, full, ring_size, piece, gain, unembedding, old_acc, old_ss, targets, *refs):
    logits_out, stats_out, scaled_out = refs[-3:]
    rows = piece.shape[0]
    span = pl.ds(e * rows, rows)
    accs, sums = [None], [None]
    ids = [block_index(ring_size, ring_size - 1, True)]
    add_blocks(ids, [piece], [span], gain, unembedding, accs, sums, scaled_out)
    square_sum = jnp.sum(old_ss[...] + sums[0], axis=1, keepdims=True)
    scale = lax.rsqrt(square_sum * (1.0 / full) + norm_eps)
    logits = (old_acc[...] + accs[0]) * scale
    logits_out[...] = logits
    wanted = jnp.broadcast_to(targets[...].astype(f32), (128, rows)).T[:, 0:1]
    hit = target_mask(wanted, logits.shape)
    target = jnp.sum(jnp.where(hit, logits, 0.0), axis=1, keepdims=True)
    top = jnp.max(logits, axis=1, keepdims=True)
    total = jnp.sum(jnp.exp(logits - top), axis=1, keepdims=True)
    lane = lax.broadcasted_iota(jnp.int32, (rows, 128), 1)
    packed = jnp.where(
        lane == 0, top, jnp.where(lane == 1, total, jnp.where(lane == 2, target, scale))
    )
    packed = jnp.where(lane == 4, wanted, packed)
    stats_out[...] = packed.T[:8, :]


def last_block(e, exits, state, scaled, ring_size, piece, targets, gain, unembedding):
    rows, width = piece.shape
    full, vocab = unembedding.shape
    args = [piece, gain, in_vmem(unembedding), *state, targets, in_vmem(scaled)]
    n = len(args)
    return call(
        functools.partial(last_kernel, e, full, ring_size),
        "last_block",
        [
            jax.ShapeDtypeStruct((rows, vocab), f32),
            jax.ShapeDtypeStruct((8, rows), f32),
            pltpu.VMEM(scaled.shape, bf16),
        ],
        [vmem_spec] * n,
        [vmem_spec, vmem_spec, vmem_spec],
        input_output_aliases={n - 1: 2},
    )(*args)


def merge_kernel(n, *refs):
    out = refs[-1]
    rows = refs[0].shape[1]
    for k in range(n):
        a, b = refs[2 * k], refs[2 * k + 1]
        top_a, top_b = a[0:1, :], b[0:1, :]
        top = jnp.maximum(top_a, top_b)
        total = a[1:2, :] * jnp.exp(top_a - top) + b[1:2, :] * jnp.exp(top_b - top)
        target = a[2:3, :] + b[2:3, :]
        row = lax.broadcasted_iota(jnp.int32, (out.shape[0], rows), 0)
        merged = jnp.where(row == 0, top, jnp.where(row == 1, total, target))
        merged = jnp.where(row > 2, a[...], merged)
        out[:, k * rows : (k + 1) * rows] = merged


def merge(*pairs):
    rows = pairs[0][0].shape[1]
    shape = jax.ShapeDtypeStruct((8, len(pairs) * rows), f32)
    kernel = functools.partial(merge_kernel, len(pairs))
    args = [x for pair in pairs for x in pair]
    return call(kernel, "merge_stats", shape, [vmem_spec] * len(args), vmem_spec)(*args)


def exit_grads(e, values, stats, exit_scale):
    rows = values.shape[0]
    cols = slice(e * rows, (e + 1) * rows)
    weight = exit_scale[0:1, e : e + 1]
    log_total = stats[0:1, cols] + jnp.log(stats[1:2, cols])
    loss = weight * jnp.sum(log_total - stats[2:3, cols], axis=1, keepdims=True)
    factor = stats[3:4, cols] * weight
    row = lax.broadcasted_iota(jnp.int32, (128, rows), 0)
    turned = jnp.where(row == 0, log_total, jnp.where(row == 1, factor, stats[4:5, cols])).T
    hit = target_mask(turned[:, 2:3], values.shape)
    soft = jnp.exp(values - turned[:, 0:1]) - jnp.where(hit, 1.0, 0.0)
    return (soft * turned[:, 1:2]).astype(bf16), loss


def grad_kernel(exits, *refs):
    logits, (stats, exit_scale, grad_out, loss_out) = refs[:exits], refs[exits:]
    rows = logits[0].shape[0]
    total = jnp.zeros((1, 1), f32)
    for e in range(exits):
        grads, loss = exit_grads(e, logits[e][...], stats, exit_scale)
        grad_out[e * rows : (e + 1) * rows, :] = grads
        total = total + loss
    loss_out[...] = jnp.broadcast_to(total, loss_out.shape)


def row_grads(logits, stats, exit_scale):
    exits = len(logits)
    rows, vocab = logits[0].shape
    return call(
        functools.partial(grad_kernel, exits),
        "row_grads",
        [jax.ShapeDtypeStruct((exits * rows, vocab), bf16), jax.ShapeDtypeStruct((8, 128), f32)],
        [vmem_spec] * (exits + 2),
        [vmem_spec, vmem_spec],
    )(*logits, stats, exit_scale)


def block_kernel(has_added, high_flip, away, units, unit, scaled, grads, *refs):
    out = refs[-1]
    group = lax.axis_index("dp")
    low = group & 1
    share = ((group >> 1) ^ high_flip) * 2 + (1 - low if away else low)
    if unit == "crossed":
        unit = 1 - (lax.axis_index("vocab") & 1)
    elif unit == "own":
        unit = lax.axis_index("vocab") & 1
    block = share * units + unit
    total = jnp.dot(scaled[block], grads[...], preferred_element_type=f32)
    if has_added:
        total = total + refs[0][...].astype(f32)
    out[...] = total.astype(out.dtype)


def grad_block(high_flip, away, units, unit, scaled, grads, added, dtype):
    width, vocab = scaled.shape[1], grads.shape[1]
    args = [in_vmem(scaled), grads] + ([] if added is None else [added])
    return call(
        functools.partial(block_kernel, added is not None, high_flip, away, units, unit),
        "grad_block",
        jax.ShapeDtypeStruct((width, vocab), dtype),
        [vmem_spec] * len(args),
        vmem_spec,
    )(*args)


def sum_kernel(units, tiles, n, count, *refs):
    parts, (loss, other, out, mean, buf, sems) = refs[: n * units], refs[n * units :]
    mean[...] = (loss[0:1, 0:1] + other[0:1, 0:1]) * (1.0 / count)
    height = parts[0].shape[0]
    tile = height // tiles
    copies = []
    for unit in range(units):
        for t in range(tiles):
            span = slice(t * tile, (t + 1) * tile)
            to = pl.ds(unit * height + t * tile, tile)
            total = parts[unit][span, :]
            for k in range(1, n):
                total = total + parts[k * units + unit][span, :].astype(f32)
            buf[to, :] = total
            copies.append(
                pltpu.make_async_copy(buf.at[to], out.at[to], sems.at[unit * tiles + t])
            )
            copies[-1].start()
    for copy in copies:
        copy.wait()


def sum_units(lists, loss, other, count):
    units = len(lists[0])
    height, vocab = lists[0][0].shape
    tiles = max(1, height // 256)
    return call(
        functools.partial(sum_kernel, units, tiles, len(lists), count),
        "sum_units",
        [
            jax.ShapeDtypeStruct((units * height, vocab), f32),
            jax.ShapeDtypeStruct((1, 1), f32),
        ],
        [vmem_spec] * (units * len(lists) + 2),
        [hbm_spec, vmem_spec],
        scratch_shapes=[
            pltpu.VMEM((units * height, vocab), f32),
            pltpu.SemaphoreType.DMA((units * tiles,)),
        ],
    )(*[part for parts in lists for part in parts], loss, other)


def own_kernel(exits, count, *refs):
    logits, refs = refs[: 2 * exits], refs[2 * exits :]
    stats, refs = refs[:2], refs[2:]
    exit_scale, *pulled, scaled, grads, came, loss, loss_core = refs[:8]
    out, part, mean, buf, sem = refs[8:]
    rows = logits[0].shape[0]
    height = buf.shape[0]
    side = lax.axis_index("vocab") & 1
    block = lax.axis_index("dp") * 2
    total = jnp.dot(scaled[block + side], grads[...], preferred_element_type=f32)
    total = total + came[pl.ds(pl.multiple_of(side * height, height), height), :].astype(f32)
    total_loss = loss[0:1, 0:1] + loss_core[0:1, 0:1]
    for k in range(2):
        for e in range(exits):
            values = logits[k * exits + e][...]
            other, loss_part = exit_grads(e, values, stats[k], exit_scale)
            total_loss = total_loss + loss_part
            rows_of = pulled[k][:, e * rows : (e + 1) * rows]
            total = total + jnp.dot(rows_of, other, preferred_element_type=f32)
    buf[...] = total
    to = pl.ds(pl.multiple_of(side * height, height), height)
    copy = pltpu.make_async_copy(buf, out.at[to], sem)
    copy.start()
    mean[...] = total_loss * (1.0 / count)
    crossed = jnp.dot(scaled[block + 1 - side], grads[...], preferred_element_type=f32)
    other_side = pl.multiple_of((1 - side) * height, height)
    part[...] = crossed + came[pl.ds(other_side, height), :].astype(f32)
    copy.wait()


def away_kernel(scaled, grads, out):
    group = lax.axis_index("dp")
    block = ((group >> 1) * 2 + 1 - (group & 1)) * 2
    width = scaled.shape[1]
    for unit in range(2):
        part = jnp.dot(scaled[block + unit], grads[...], preferred_element_type=f32)
        out[unit * width : (unit + 1) * width, :] = part.astype(bf16)


def away_share(scaled, grads):
    width, vocab = scaled.shape[1], grads.shape[1]
    shape = jax.ShapeDtypeStruct((2 * width, vocab), bf16)
    return call(away_kernel, "away_share", shape, [vmem_spec] * 2, vmem_spec)(in_vmem(scaled), grads)


def own_block(logits, stats, exit_scale, pulled, scaled, grads, came, losses, count):
    exits = exit_scale.shape[1]
    height, vocab = came.shape[0] // 2, came.shape[1]
    args = [*logits, *stats, exit_scale, *pulled, in_vmem(scaled), grads, came, *losses]
    return call(
        functools.partial(own_kernel, exits, count),
        "own_block",
        [
            jax.ShapeDtypeStruct((2 * height, vocab), f32),
            jax.ShapeDtypeStruct((height, vocab), f32),
            jax.ShapeDtypeStruct((1, 1), f32),
        ],
        [vmem_spec] * len(args),
        [hbm_spec, vmem_spec, vmem_spec],
        scratch_shapes=[pltpu.VMEM((height, vocab), f32), pltpu.SemaphoreType.DMA],
    )(*args)


def crossed_kernel(tiles, part, over, _, out, buf, sems):
    height = part.shape[0]
    tile = height // tiles
    start = (1 - (lax.axis_index("vocab") & 1)) * height
    copies = []
    for t in range(tiles):
        span = slice(t * tile, (t + 1) * tile)
        buf[span, :] = part[span, :] + over[span, :].astype(f32)
        to = pl.ds(pl.multiple_of(start + t * tile, tile), tile)
        copies.append(pltpu.make_async_copy(buf.at[pl.ds(t * tile, tile)], out.at[to], sems.at[t]))
        copies[t].start()
    for copy in copies:
        copy.wait()


def crossed_block(part, over, out):
    height, vocab = part.shape
    tiles = max(1, height // 256)
    return call(
        functools.partial(crossed_kernel, tiles),
        "crossed_block",
        jax.ShapeDtypeStruct(out.shape, f32),
        [vmem_spec, vmem_spec, hbm_spec],
        hbm_spec,
        input_output_aliases={2: 0},
        scratch_shapes=[pltpu.VMEM((height, vocab), f32), pltpu.SemaphoreType.DMA((tiles,))],
    )(part, over, out)


def flip(axis, bit):
    return [(i, i ^ bit) for i in range(lax.axis_size(axis))]


def per_device(hidden_states, exit_layers, targets, norm_gain, exit_scale, unembedding):
    exits = exit_layers.shape[1]
    tokens = hidden_states.shape[1]
    full, vocab_local = unembedding.shape
    n_vocab, n_dp = lax.axis_size("vocab"), lax.axis_size("dp")
    ring_size = n_vocab // 2
    ring = [(j, (j + 2) % n_vocab) for j in range(n_vocab)]
    pair = flip("vocab", 1)
    layers = exit_layers.T
    gain = norm_gain.astype(f32).reshape(n_vocab, full // n_vocab)
    target_row = targets.reshape(1, tokens)

    paired = n_dp == 4 and n_vocab == 2 * n_dp

    def pull_pairs(step):
        pairs = []
        for d in range(n_dp):
            for j in range(n_vocab):
                if (j // 2 - step) % ring_size // 2 != d // 2:
                    pairs.append((d * n_vocab + j, (d ^ 2) * n_vocab + j))
        return pairs

    states, scaled = [None] * exits, None
    current = [select(hidden_states, layers, e) for e in range(exits)]
    crossed, pulled, pending = None, None, None
    for step in range(ring_size):
        last = step == ring_size - 1
        crossing, coming = [], []
        for e in range(exits):
            piece = current[e]
            if crossed is not None:
                before = (e - 1) % exits
                piece, crossed[e], states[before] = bar((piece, crossed[e], states[before]))
            elif e:
                piece, states[e - 1] = bar((piece, states[e - 1]))
            if not last:
                coming.append(lax.ppermute(piece, "vocab", ring))
            if last and step > 0 and e >= exits // 2:
                crossing.append(lax.ppermute(crossed[e], "vocab", ring))
            else:
                crossing.append(lax.ppermute(piece, "vocab", pair))
            sent = lax.ppermute(piece, ("dp", "vocab"), pull_pairs(step)) if paired else None
            if pending is not None:
                piece, came = bar((piece, pending[2]))
                pulled = pull(pulled, pending[1], exits, ring_size, pending[0], came, gain)
            pending = (step, e, sent) if paired else None
            pieces = [piece] if crossed is None else [piece, crossed[e]]
            states[e], scaled = arrival(
                states[e], scaled, e, exits, ring_size, step, pieces, gain, unembedding
            )
        crossed, current = crossing, coming

    def over_y(x):
        return lax.ppermute(x, "dp", flip("dp", 2))

    def over_core(x):
        return lax.ppermute(x, "dp", flip("dp", 1))

    logits, own_stats, partner_stats = [], [], []
    for e in range(exits):
        if e:
            crossed[e], partner_stats[e - 1] = bar((crossed[e], partner_stats[e - 1]))
        values, stats, scaled = last_block(
            e, exits, states[e], scaled, ring_size, crossed[e], target_row, gain, unembedding
        )
        logits.append(values)
        own_stats.append(stats)
        partner_stats.append(lax.ppermute(stats, "vocab", pair))
    stats = merge(*zip(own_stats, partner_stats))
    scale_row = exit_scale.reshape(1, exits)
    if paired:
        y_logits = [over_y(values) for values in logits]
    bit = 2
    while bit < n_vocab:
        if 2 * bit == n_vocab and paired:
            stats, came, pulled = bar((stats, pending[2], pulled))
        stats = merge((stats, lax.ppermute(stats, "vocab", flip("vocab", bit))))
        bit *= 2
    if paired:
        stats, y_logits = bar((stats, y_logits))
        y_stats = over_y(stats)
        pulled = pull(pulled, pending[1], exits, ring_size, pending[0], came, gain)
        y_logits, pulled = bar((y_logits, pulled, y_stats))[:2]
        yc_logits = [over_core(values) for values in y_logits]
        pulled = (pulled[0], over_core(pulled[1]))
    grads, loss = row_grads(logits, stats, scale_row)

    if paired:
        came = over_core(grad_block(1, True, 2, "crossed", scaled, grads, None, bf16))
        came, share = bar((came, away_share(scaled, grads)))
        home = grad_block(1, False, 2, "crossed", scaled, grads, came, bf16)
        over = over_y(home)
        came = over_core(share)
        weight_grad, part, mean_loss = own_block(
            y_logits + yc_logits, (y_stats, over_core(y_stats)), scale_row,
            pulled, scaled, grads, came, (loss, over_core(loss)), tokens * n_dp,
        )
        return (crossed_block(part, over, weight_grad), mean_loss.reshape(()))

    n_high = n_dp // 2
    units = n_vocab // n_dp
    held = {}
    for high_flip in reversed(range(n_high)):
        came = []
        for unit in range(units):
            away = grad_block(high_flip, True, units, unit, scaled, grads, None, bf16)
            came.append(lax.ppermute(away, "dp", flip("dp", 1)))
        for unit in range(units):
            held[high_flip, unit] = grad_block(
                high_flip, False, units, unit, scaled, grads,
                came[unit] if high_flip else None, bf16 if high_flip else f32,
            )
        if high_flip:
            grads, loss = bar((grads, loss, *[held[high_flip, unit] for unit in range(units)]))[:2]
    bit = 1
    while bit < n_high:
        loss = loss + lax.ppermute(loss, "dp", flip("dp", bit))
        bit *= 2
    other_loss = lax.ppermute(loss, "dp", flip("dp", bit))
    bit = 1
    while bit < n_high:
        kept = {}
        for h in reversed(range(0, n_high, 2 * bit)):
            over = [
                lax.ppermute(held[h + bit, unit], "dp", flip("dp", 2 * bit)) for unit in range(units)
            ]
            if 2 * bit == n_high:
                parts = [[held[0, unit] for unit in range(units)], came, over]
                weight_grad, mean_loss = sum_units(parts, loss, other_loss, tokens * n_dp)
            else:
                for unit in range(units):
                    total = held[h, unit].astype(f32) + over[unit].astype(f32)
                    kept[h, unit] = total.astype(bf16) if h else total
        held = kept
        bit *= 2
    return (weight_grad, mean_loss.reshape(()))


def solution(mesh):
    in_specs = (P(None, "dp", "vocab"), P("dp", None), P("dp"), P(), P(), P(None, "vocab"))
    out_specs = (P("dp", "vocab"), P())
    return jax.shard_map(
        per_device, mesh=mesh, in_specs=in_specs, out_specs=out_specs, check_vma=False
    )
```

```python
import functools

import jax
import jax.numpy as jnp
from jax import lax
from jax.experimental import pallas as pl
from jax.experimental.pallas import tpu as pltpu
from jax.sharding import PartitionSpec as P

norm_eps = 1e-05
f32, bf16 = jnp.float32, jnp.bfloat16
vmem_bytes = 16 * 1024 * 1024
bar = lax.optimization_barrier
smem_spec = pl.BlockSpec(memory_space=pltpu.SMEM)
hbm_spec = pl.BlockSpec(memory_space=pltpu.HBM)
vmem_spec = pl.BlockSpec(memory_space=pltpu.VMEM)


def in_hbm(x):
    return pltpu.with_memory_space_constraint(x, pltpu.HBM)


def in_vmem(x):
    return pltpu.with_memory_space_constraint(x, pltpu.VMEM)


def call(kernel, name, out_shape, in_specs, out_specs, **more):
    return pl.pallas_call(
        kernel,
        name=name,
        out_shape=out_shape,
        in_specs=in_specs,
        out_specs=out_specs,
        compiler_params=pltpu.CompilerParams(vmem_limit_bytes=vmem_bytes),
        **more,
    )


def select_kernel(exit_index, row_len, layers_ref, hidden_ref, out_ref, layers, layers_sem, sems):
    load = pltpu.make_async_copy(layers_ref, layers, layers_sem)
    load.start()
    load.wait()
    copies = []
    for r in range(layers.shape[1]):
        span = pl.ds(r * row_len, row_len)
        source = hidden_ref.at[layers[exit_index, r], span]
        copies.append(pltpu.make_async_copy(source, out_ref.at[span], sems.at[r]))
    for copy in copies:
        copy.start()
    for copy in copies:
        copy.wait()


def select(hidden, layers, exit_index):
    _, tokens, width = hidden.shape
    rows = layers.shape[1]
    return call(
        functools.partial(select_kernel, exit_index, tokens // rows),
        "select_rows",
        jax.ShapeDtypeStruct((tokens, width), hidden.dtype),
        [hbm_spec, hbm_spec],
        pl.BlockSpec(memory_space=pl.ANY),
        scratch_shapes=[
            pltpu.SMEM(layers.shape, jnp.int32),
            pltpu.SemaphoreType.DMA,
            pltpu.SemaphoreType.DMA((rows,)),
        ],
    )(in_hbm(layers), in_hbm(hidden))


def owner_index(ring_size, step):
    return lax.rem((lax.axis_index("vocab") >> 1) + (ring_size - step), jnp.int32(ring_size))


def block_index(ring_size, step, crossed):
    side = lax.axis_index("vocab") & 1
    return owner_index(ring_size, step) * 2 + (1 - side if crossed else side)


def add_blocks(ids, pieces, spans, gain, unembedding, accs, sums, scaled_out):
    width = pieces[0].shape[1]
    lanes = min(128, width)
    for p in range(len(pieces)):
        x = pieces[p][...].astype(f32)
        scaled = (x * gain[pl.ds(ids[p], 1), :]).astype(bf16)
        scaled_out[ids[p], :, spans[p]] = scaled.T
        weights = unembedding[pl.ds(pl.multiple_of(ids[p] * width, width), width), :]
        accs[p] = jnp.dot(scaled, weights, preferred_element_type=f32)
        square = x * x
        total = square[:, :lanes]
        for start in range(lanes, width, lanes):
            total = total + square[:, start : start + lanes]
        sums[p] = total


def arrival_kernel(n, first, makes, exit_index, ring_size, step, *refs):
    ids = [block_index(ring_size, step - p, p == 1) for p in range(n)]
    pieces, refs = refs[:n], refs[n:]
    gain, unembedding = refs[:2]
    refs = refs[2:]
    if not first:
        acc, ss = refs[:2]
        refs = refs[2:]
    if not makes:
        refs = refs[1:]
    acc_out, ss_out, scaled_out = refs
    rows = pieces[0].shape[0]
    span = pl.ds(exit_index * rows, rows)
    accs, sums = [None] * n, [None] * n
    add_blocks(ids, pieces, [span] * n, gain, unembedding, accs, sums, scaled_out)
    total, squares = accs[0], sums[0]
    for p in range(1, n):
        total, squares = total + accs[p], squares + sums[p]
    if not first:
        total, squares = total + acc[...], squares + ss[...]
    acc_out[...] = total
    ss_out[...] = squares


def arrival(state, scaled, exit_index, exits, ring_size, step, pieces, gain, unembedding):
    rows, width = pieces[0].shape
    full, vocab = unembedding.shape
    lanes = min(128, width)
    n = len(pieces)
    first, makes = state is None, scaled is None
    args = [*pieces, gain, in_vmem(unembedding)]
    specs = [vmem_spec] * (n + 2)
    aliases = {}
    if not first:
        aliases = {len(args): 0, len(args) + 1: 1}
        args += list(state)
        specs += [vmem_spec, vmem_spec]
    if not makes:
        aliases[len(args)] = 2
        args.append(in_vmem(scaled))
        specs.append(vmem_spec)
    acc, ss, scaled = call(
        functools.partial(arrival_kernel, n, first, makes, exit_index, ring_size, step),
        "arrival",
        [
            jax.ShapeDtypeStruct((rows, vocab), f32),
            jax.ShapeDtypeStruct((rows, lanes), f32),
            pltpu.VMEM((full // width, width, exits * rows), bf16),
        ],
        specs,
        [vmem_spec, vmem_spec, vmem_spec],
        input_output_aliases=aliases,
    )(*args)
    return (acc, ss), scaled


def pull_kernel(ring_size, step, e, *refs):
    piece, gain, (own_out, relay_out) = refs[0], refs[1], refs[-2:]
    rows = piece.shape[0]
    owner, group = owner_index(ring_size, step), lax.axis_index("dp")

    @pl.when((owner >> 1) == (group >> 1))
    def _():
        block = owner * 2 + (lax.axis_index("vocab") & 1)
        x = piece[...].astype(f32) * gain[pl.ds(block, 1), :]
        turned = x.astype(bf16).T

        @pl.when(owner == group)
        def _():
            own_out[:, e * rows : (e + 1) * rows] = turned

        @pl.when(owner != group)
        def _():
            relay_out[:, e * rows : (e + 1) * rows] = turned


def pull(pulled, e, exits, ring_size, step, piece, gain):
    rows, width = piece.shape
    args = [piece, gain] + ([] if pulled is None else [in_vmem(x) for x in pulled])
    return call(
        functools.partial(pull_kernel, ring_size, step, e),
        "pull",
        [pltpu.VMEM((width, exits * rows), bf16)] * 2,
        [vmem_spec] * len(args),
        [vmem_spec] * 2,
        input_output_aliases={} if pulled is None else {2: 0, 3: 1},
    )(*args)


def target_mask(wanted, shape):
    first = (lax.axis_index("vocab") * shape[1]).astype(f32)
    return lax.broadcasted_iota(jnp.int32, shape, 1).astype(f32) + first == wanted


def split_kernel(a, b, first, second):
    count = first.shape[0]
    first[...] = a[:count, :]
    second[...] = b[count:, :]


def split_rows(a, b):
    rows, width = a.shape
    count = rows * 3 // 4
    shapes = [jax.ShapeDtypeStruct((n, width), a.dtype) for n in (count, rows - count)]
    return call(split_kernel, "split_rows", shapes, [vmem_spec] * 2, [vmem_spec] * 2)(a, b)


def last_kernel(e, full, ring_size, n, *refs):
    pieces, (gain, unembedding, old_acc, old_ss, targets) = refs[:n], refs[n : n + 5]
    logits_out, weights_out, stats_out, scaled_out = refs[-4:]
    rows = old_acc.shape[0]
    piece = jnp.concatenate([p[...] for p in pieces], axis=0) if n > 1 else pieces[0]
    span = pl.ds(e * rows, rows)
    accs, sums = [None], [None]
    ids = [block_index(ring_size, ring_size - 1, True)]
    add_blocks(ids, [piece], [span], gain, unembedding, accs, sums, scaled_out)
    square_sum = jnp.sum(old_ss[...] + sums[0], axis=1, keepdims=True)
    scale = lax.rsqrt(square_sum * (1.0 / full) + norm_eps)
    logits = (old_acc[...] + accs[0]) * scale
    logits_out[...] = logits
    wanted = jnp.broadcast_to(targets[...].astype(f32), (128, rows)).T[:, 0:1]
    hit = target_mask(wanted, logits.shape)
    target = jnp.sum(jnp.where(hit, logits, 0.0), axis=1, keepdims=True)
    top = jnp.max(logits, axis=1, keepdims=True)
    weights = jnp.exp(logits - top)
    weights_out[span, :] = weights.astype(bf16)
    total = jnp.sum(weights, axis=1, keepdims=True)
    lane = lax.broadcasted_iota(jnp.int32, (rows, 128), 1)
    packed = jnp.where(
        lane == 0, top, jnp.where(lane == 1, total, jnp.where(lane == 2, target, scale))
    )
    packed = jnp.where(lane == 4, wanted, jnp.where(lane == 5, top, packed))
    stats_out[:, e * rows : (e + 1) * rows] = packed.T[:8, :]


def last_block(e, exits, made, state, scaled, ring_size, pieces, targets, gain, unembedding):
    rows = state[0].shape[0]
    full, vocab = unembedding.shape
    args = [*pieces, gain, in_vmem(unembedding), *state, targets]
    args += [*made, in_vmem(scaled)]
    n = len(args)
    aliases = {n - 1: 3, n - 2: 2, n - 3: 1} if made else {n - 1: 3}
    return call(
        functools.partial(last_kernel, e, full, ring_size, len(pieces)),
        "last_block",
        [
            jax.ShapeDtypeStruct((rows, vocab), f32),
            jax.ShapeDtypeStruct((exits * rows, vocab), bf16),
            jax.ShapeDtypeStruct((8, exits * rows), f32),
            pltpu.VMEM(scaled.shape, bf16),
        ],
        [vmem_spec] * n,
        [vmem_spec] * 4,
        input_output_aliases=aliases,
    )(*args)


def merge_kernel(n, *refs):
    out = refs[-1]
    rows = refs[0].shape[1]
    for k in range(n):
        a, b = refs[2 * k], refs[2 * k + 1]
        top_a, top_b = a[0:1, :], b[0:1, :]
        top = jnp.maximum(top_a, top_b)
        total = a[1:2, :] * jnp.exp(top_a - top) + b[1:2, :] * jnp.exp(top_b - top)
        target = a[2:3, :] + b[2:3, :]
        row = lax.broadcasted_iota(jnp.int32, (out.shape[0], rows), 0)
        merged = jnp.where(row == 0, top, jnp.where(row == 1, total, target))
        merged = jnp.where(row > 2, a[...], merged)
        out[:, k * rows : (k + 1) * rows] = merged


def merge(*pairs):
    rows = pairs[0][0].shape[1]
    shape = jax.ShapeDtypeStruct((8, len(pairs) * rows), f32)
    kernel = functools.partial(merge_kernel, len(pairs))
    args = [x for pair in pairs for x in pair]
    return call(kernel, "merge_stats", shape, [vmem_spec] * len(args), vmem_spec)(*args)


def exit_rows(e, rows, stats, exit_scale):
    cols = slice(e * rows, (e + 1) * rows)
    weight = exit_scale[0:1, e : e + 1]
    log_total = stats[0:1, cols] + jnp.log(stats[1:2, cols])
    target = stats[2:3, cols]
    loss = weight * jnp.sum(log_total - target, axis=1, keepdims=True)
    return log_total, target, stats[3:4, cols] * weight, loss


def turn(rows, first, second, third):
    row = lax.broadcasted_iota(jnp.int32, (128, rows), 0)
    turned = jnp.where(row == 0, first, jnp.where(row == 1, second, third)).T
    return turned[:, 0:1], turned[:, 1:2], turned[:, 2:3]


def exit_grads(e, values, stats, exit_scale):
    rows = values.shape[0]
    log_total, _, factor, loss = exit_rows(e, rows, stats, exit_scale)
    wanted = stats[4:5, e * rows : (e + 1) * rows]
    log_total, factor, wanted = turn(rows, log_total, factor, wanted)
    hit = target_mask(wanted, values.shape)
    soft = jnp.exp(values - log_total) - jnp.where(hit, 1.0, 0.0)
    return (soft * factor).astype(bf16), loss


def exit_grads_of(e, weights, stats, exit_scale):
    rows = weights.shape[0]
    log_total, target, factor, loss = exit_rows(e, rows, stats, exit_scale)
    cols = slice(e * rows, (e + 1) * rows)
    others = jnp.exp(stats[5:6, cols] - log_total) * factor
    at_target = (jnp.exp(target - log_total) - 1.0) * factor
    others, at_target, wanted = turn(rows, others, at_target, stats[4:5, cols])
    hit = target_mask(wanted, weights.shape)
    return jnp.where(hit, at_target, weights.astype(f32) * others).astype(bf16), loss


def grad_kernel(exits, *refs):
    logits, (stats, exit_scale, grad_out, loss_out) = refs[:exits], refs[exits:]
    rows = logits[0].shape[0]
    total = jnp.zeros((1, 1), f32)
    for e in range(exits):
        grads, loss = exit_grads(e, logits[e][...], stats, exit_scale)
        grad_out[e * rows : (e + 1) * rows, :] = grads
        total = total + loss
    loss_out[...] = jnp.broadcast_to(total, loss_out.shape)


def row_grads(logits, stats, exit_scale):
    exits = len(logits)
    rows, vocab = logits[0].shape
    return call(
        functools.partial(grad_kernel, exits),
        "row_grads",
        [jax.ShapeDtypeStruct((exits * rows, vocab), bf16), jax.ShapeDtypeStruct((8, 128), f32)],
        [vmem_spec] * (exits + 2),
        [vmem_spec, vmem_spec],
    )(*logits, stats, exit_scale)


def block_kernel(has_added, high_flip, away, units, unit, scaled, grads, *refs):
    out = refs[-1]
    group = lax.axis_index("dp")
    low = group & 1
    share = ((group >> 1) ^ high_flip) * 2 + (1 - low if away else low)
    if unit == "crossed":
        unit = 1 - (lax.axis_index("vocab") & 1)
    elif unit == "own":
        unit = lax.axis_index("vocab") & 1
    block = share * units + unit
    total = jnp.dot(scaled[block], grads[...], preferred_element_type=f32)
    if has_added:
        total = total + refs[0][...].astype(f32)
    out[...] = total.astype(out.dtype)


def grad_block(high_flip, away, units, unit, scaled, grads, added, dtype):
    width, vocab = scaled.shape[1], grads.shape[1]
    args = [in_vmem(scaled), grads] + ([] if added is None else [added])
    return call(
        functools.partial(block_kernel, added is not None, high_flip, away, units, unit),
        "grad_block",
        jax.ShapeDtypeStruct((width, vocab), dtype),
        [vmem_spec] * len(args),
        vmem_spec,
    )(*args)


def sum_kernel(units, tiles, n, count, *refs):
    parts, (loss, other, out, mean, buf, sems) = refs[: n * units], refs[n * units :]
    mean[...] = (loss[0:1, 0:1] + other[0:1, 0:1]) * (1.0 / count)
    height = parts[0].shape[0]
    tile = height // tiles
    copies = []
    for unit in range(units):
        for t in range(tiles):
            span = slice(t * tile, (t + 1) * tile)
            to = pl.ds(unit * height + t * tile, tile)
            total = parts[unit][span, :]
            for k in range(1, n):
                total = total + parts[k * units + unit][span, :].astype(f32)
            buf[to, :] = total
            copies.append(
                pltpu.make_async_copy(buf.at[to], out.at[to], sems.at[unit * tiles + t])
            )
            copies[-1].start()
    for copy in copies:
        copy.wait()


def sum_units(lists, loss, other, count):
    units = len(lists[0])
    height, vocab = lists[0][0].shape
    tiles = max(1, height // 256)
    return call(
        functools.partial(sum_kernel, units, tiles, len(lists), count),
        "sum_units",
        [
            jax.ShapeDtypeStruct((units * height, vocab), f32),
            jax.ShapeDtypeStruct((1, 1), f32),
        ],
        [vmem_spec] * (units * len(lists) + 2),
        [hbm_spec, vmem_spec],
        scratch_shapes=[
            pltpu.VMEM((units * height, vocab), f32),
            pltpu.SemaphoreType.DMA((units * tiles,)),
        ],
    )(*[part for parts in lists for part in parts], loss, other)


def own_kernel(exits, count, *refs):
    weights, refs = refs[:2], refs[2:]
    stats, refs = refs[:2], refs[2:]
    exit_scale, *pulled, scaled, grads, came, loss, loss_core = refs[:8]
    out, part, mean, buf, sem = refs[8:]
    rows = weights[0].shape[0] // exits
    height = buf.shape[0]
    side = lax.axis_index("vocab") & 1
    block = lax.axis_index("dp") * 2
    total = jnp.dot(scaled[block + side], grads[...], preferred_element_type=f32)
    total = total + came[pl.ds(pl.multiple_of(side * height, height), height), :].astype(f32)
    total_loss = loss[0:1, 0:1] + loss_core[0:1, 0:1]
    for k in range(2):
        for e in range(exits):
            values = weights[k][e * rows : (e + 1) * rows, :]
            other, loss_part = exit_grads_of(e, values, stats[k], exit_scale)
            total_loss = total_loss + loss_part
            rows_of = pulled[k][:, e * rows : (e + 1) * rows]
            total = total + jnp.dot(rows_of, other, preferred_element_type=f32)
    buf[...] = total
    to = pl.ds(pl.multiple_of(side * height, height), height)
    copy = pltpu.make_async_copy(buf, out.at[to], sem)
    copy.start()
    mean[...] = total_loss * (1.0 / count)
    crossed = jnp.dot(scaled[block + 1 - side], grads[...], preferred_element_type=f32)
    other_side = pl.multiple_of((1 - side) * height, height)
    part[...] = crossed + came[pl.ds(other_side, height), :].astype(f32)
    copy.wait()


def away_kernel(scaled, grads, out):
    group = lax.axis_index("dp")
    block = ((group >> 1) * 2 + 1 - (group & 1)) * 2
    width = scaled.shape[1]
    for unit in range(2):
        part = jnp.dot(scaled[block + unit], grads[...], preferred_element_type=f32)
        out[unit * width : (unit + 1) * width, :] = part.astype(bf16)


def away_share(scaled, grads):
    width, vocab = scaled.shape[1], grads.shape[1]
    shape = jax.ShapeDtypeStruct((2 * width, vocab), bf16)
    return call(away_kernel, "away_share", shape, [vmem_spec] * 2, vmem_spec)(in_vmem(scaled), grads)


def own_block(weights, stats, exit_scale, pulled, scaled, grads, came, losses, count):
    exits = exit_scale.shape[1]
    height, vocab = came.shape[0] // 2, came.shape[1]
    args = [*weights, *stats, exit_scale, *pulled, in_vmem(scaled), grads, came, *losses]
    return call(
        functools.partial(own_kernel, exits, count),
        "own_block",
        [
            jax.ShapeDtypeStruct((2 * height, vocab), f32),
            jax.ShapeDtypeStruct((height, vocab), f32),
            jax.ShapeDtypeStruct((1, 1), f32),
        ],
        [vmem_spec] * len(args),
        [hbm_spec, vmem_spec, vmem_spec],
        scratch_shapes=[pltpu.VMEM((height, vocab), f32), pltpu.SemaphoreType.DMA],
    )(*args)


def crossed_kernel(tiles, part, over, _, out, buf, sems):
    height = part.shape[0]
    tile = height // tiles
    start = (1 - (lax.axis_index("vocab") & 1)) * height
    copies = []
    for t in range(tiles):
        span = slice(t * tile, (t + 1) * tile)
        buf[span, :] = part[span, :] + over[span, :].astype(f32)
        to = pl.ds(pl.multiple_of(start + t * tile, tile), tile)
        copies.append(pltpu.make_async_copy(buf.at[pl.ds(t * tile, tile)], out.at[to], sems.at[t]))
        copies[t].start()
    for copy in copies:
        copy.wait()


def crossed_block(part, over, out):
    height, vocab = part.shape
    tiles = max(1, height // 256)
    return call(
        functools.partial(crossed_kernel, tiles),
        "crossed_block",
        jax.ShapeDtypeStruct(out.shape, f32),
        [vmem_spec, vmem_spec, hbm_spec],
        hbm_spec,
        input_output_aliases={2: 0},
        scratch_shapes=[pltpu.VMEM((height, vocab), f32), pltpu.SemaphoreType.DMA((tiles,))],
    )(part, over, out)


def flip(axis, bit):
    return [(i, i ^ bit) for i in range(lax.axis_size(axis))]


def per_device(hidden_states, exit_layers, targets, norm_gain, exit_scale, unembedding):
    exits = exit_layers.shape[1]
    tokens = hidden_states.shape[1]
    full, vocab_local = unembedding.shape
    n_vocab, n_dp = lax.axis_size("vocab"), lax.axis_size("dp")
    ring_size = n_vocab // 2
    ring = [(j, (j + 2) % n_vocab) for j in range(n_vocab)]
    pair = flip("vocab", 1)
    layers = exit_layers.T
    gain = norm_gain.astype(f32).reshape(n_vocab, full // n_vocab)
    target_row = targets.reshape(1, tokens)

    paired = n_dp == 4 and n_vocab == 2 * n_dp

    def pull_pairs(step):
        pairs = []
        for d in range(n_dp):
            for j in range(n_vocab):
                if (j // 2 - step) % ring_size // 2 != d // 2:
                    pairs.append((d * n_vocab + j, (d ^ 2) * n_vocab + j))
        return pairs

    states, scaled = [None] * exits, None
    current = [select(hidden_states, layers, e) for e in range(exits)]
    crossed, pulled, pending = None, None, None
    for step in range(ring_size):
        last = step == ring_size - 1
        crossing, coming = [], []
        for e in range(exits):
            piece = current[e]
            if crossed is not None:
                before = (e - 1) % exits
                piece, crossed[e], states[before] = bar((piece, crossed[e], states[before]))
            elif e:
                piece, states[e - 1] = bar((piece, states[e - 1]))
            if not last:
                coming.append(lax.ppermute(piece, "vocab", ring))
            if last and step > 0 and e >= exits // 2:
                from_ring, from_pair = split_rows(crossed[e], piece)
                crossing.append(
                    [lax.ppermute(from_ring, "vocab", ring), lax.ppermute(from_pair, "vocab", pair)]
                )
            else:
                crossed_piece = lax.ppermute(piece, "vocab", pair)
                crossing.append([crossed_piece] if last else crossed_piece)
            sent = lax.ppermute(piece, ("dp", "vocab"), pull_pairs(step)) if paired else None
            if pending is not None:
                piece, came = bar((piece, pending[2]))
                pulled = pull(pulled, pending[1], exits, ring_size, pending[0], came, gain)
            pending = (step, e, sent) if paired else None
            if last and e:
                piece, crossing[0] = bar((piece, crossing[0]))
            pieces = [piece] if crossed is None else [piece, crossed[e]]
            states[e], scaled = arrival(
                states[e], scaled, e, exits, ring_size, step, pieces, gain, unembedding
            )
        crossed, current = crossing, coming

    def over_y(x):
        return lax.ppermute(x, "dp", flip("dp", 2))

    def over_core(x):
        return lax.ppermute(x, "dp", flip("dp", 1))

    logits, made = [], ()
    for e in range(exits):
        values, *made, scaled = last_block(
            e, exits, made, states[e], scaled, ring_size, crossed[e], target_row, gain, unembedding
        )
        logits.append(values)
    weights, stats = made
    stats = merge((stats, lax.ppermute(stats, "vocab", pair)))
    scale_row = exit_scale.reshape(1, exits)
    if paired:
        weights, stats = bar((weights, stats))
        y_weights = over_y(weights)
    bit = 2
    while bit < n_vocab:
        if 2 * bit == n_vocab and paired:
            stats, came, pulled = bar((stats, pending[2], pulled))
        stats = merge((stats, lax.ppermute(stats, "vocab", flip("vocab", bit))))
        bit *= 2
    if paired:
        stats, y_weights = bar((stats, y_weights))
        y_stats = over_y(stats)
        pulled = pull(pulled, pending[1], exits, ring_size, pending[0], came, gain)
        y_weights, pulled = bar((y_weights, pulled, y_stats))[:2]
        yc_weights = over_core(y_weights)
        pulled = (pulled[0], over_core(pulled[1]))
    grads, loss = row_grads(logits, stats, scale_row)

    if paired:
        came = over_core(grad_block(1, True, 2, "crossed", scaled, grads, None, bf16))
        came, share = bar((came, away_share(scaled, grads)))
        home = grad_block(1, False, 2, "crossed", scaled, grads, came, bf16)
        over = over_y(home)
        came = over_core(share)
        weight_grad, part, mean_loss = own_block(
            (y_weights, yc_weights), (y_stats, over_core(y_stats)), scale_row,
            pulled, scaled, grads, came, (loss, over_core(loss)), tokens * n_dp,
        )
        return (crossed_block(part, over, weight_grad), mean_loss.reshape(()))

    n_high = n_dp // 2
    units = n_vocab // n_dp
    held = {}
    for high_flip in reversed(range(n_high)):
        came = []
        for unit in range(units):
            away = grad_block(high_flip, True, units, unit, scaled, grads, None, bf16)
            came.append(lax.ppermute(away, "dp", flip("dp", 1)))
        for unit in range(units):
            held[high_flip, unit] = grad_block(
                high_flip, False, units, unit, scaled, grads,
                came[unit] if high_flip else None, bf16 if high_flip else f32,
            )
        if high_flip:
            grads, loss = bar((grads, loss, *[held[high_flip, unit] for unit in range(units)]))[:2]
    bit = 1
    while bit < n_high:
        loss = loss + lax.ppermute(loss, "dp", flip("dp", bit))
        bit *= 2
    other_loss = lax.ppermute(loss, "dp", flip("dp", bit))
    bit = 1
    while bit < n_high:
        kept = {}
        for h in reversed(range(0, n_high, 2 * bit)):
            over = [
                lax.ppermute(held[h + bit, unit], "dp", flip("dp", 2 * bit)) for unit in range(units)
            ]
            if 2 * bit == n_high:
                parts = [[held[0, unit] for unit in range(units)], came, over]
                weight_grad, mean_loss = sum_units(parts, loss, other_loss, tokens * n_dp)
            else:
                for unit in range(units):
                    total = held[h, unit].astype(f32) + over[unit].astype(f32)
                    kept[h, unit] = total.astype(bf16) if h else total
        held = kept
        bit *= 2
    return (weight_grad, mean_loss.reshape(()))


def solution(mesh):
    in_specs = (P(None, "dp", "vocab"), P("dp", None), P("dp"), P(), P(), P(None, "vocab"))
    out_specs = (P("dp", "vocab"), P())
    return jax.shard_map(
        per_device, mesh=mesh, in_specs=in_specs, out_specs=out_specs, check_vma=False
    )
```

```python
import functools

import jax
import jax.numpy as jnp
from jax import lax
from jax.experimental import pallas as pl
from jax.experimental.pallas import tpu as pltpu
from jax.sharding import PartitionSpec as P

norm_eps = 1e-05
f32, bf16 = jnp.float32, jnp.bfloat16
vmem_bytes = 16 * 1024 * 1024
bar = lax.optimization_barrier
smem_spec = pl.BlockSpec(memory_space=pltpu.SMEM)
hbm_spec = pl.BlockSpec(memory_space=pltpu.HBM)
vmem_spec = pl.BlockSpec(memory_space=pltpu.VMEM)


def in_hbm(x):
    return pltpu.with_memory_space_constraint(x, pltpu.HBM)


def in_vmem(x):
    return pltpu.with_memory_space_constraint(x, pltpu.VMEM)


def call(kernel, name, out_shape, in_specs, out_specs, **more):
    return pl.pallas_call(
        kernel,
        name=name,
        out_shape=out_shape,
        in_specs=in_specs,
        out_specs=out_specs,
        compiler_params=pltpu.CompilerParams(vmem_limit_bytes=vmem_bytes),
        **more,
    )


def select_kernel(exit_index, row_len, layers_ref, hidden_ref, out_ref, layers, layers_sem, sems):
    load = pltpu.make_async_copy(layers_ref, layers, layers_sem)
    load.start()
    load.wait()
    copies = []
    for r in range(layers.shape[1]):
        span = pl.ds(r * row_len, row_len)
        source = hidden_ref.at[layers[exit_index, r], span]
        copies.append(pltpu.make_async_copy(source, out_ref.at[span], sems.at[r]))
    for copy in copies:
        copy.start()
    for copy in copies:
        copy.wait()


def select(hidden, layers, exit_index):
    _, tokens, width = hidden.shape
    rows = layers.shape[1]
    return call(
        functools.partial(select_kernel, exit_index, tokens // rows),
        "select_rows",
        jax.ShapeDtypeStruct((tokens, width), hidden.dtype),
        [hbm_spec, hbm_spec],
        pl.BlockSpec(memory_space=pl.ANY),
        scratch_shapes=[
            pltpu.SMEM(layers.shape, jnp.int32),
            pltpu.SemaphoreType.DMA,
            pltpu.SemaphoreType.DMA((rows,)),
        ],
    )(in_hbm(layers), in_hbm(hidden))


def owner_index(ring_size, step):
    return lax.rem((lax.axis_index("vocab") >> 1) + (ring_size - step), jnp.int32(ring_size))


def block_index(ring_size, step, crossed):
    side = lax.axis_index("vocab") & 1
    return owner_index(ring_size, step) * 2 + (1 - side if crossed else side)


def add_blocks(ids, pieces, spans, gain, unembedding, accs, sums, scaled_out):
    width = pieces[0].shape[1]
    lanes = min(128, width)
    for p in range(len(pieces)):
        x = pieces[p][...].astype(f32)
        scaled = (x * gain[pl.ds(ids[p], 1), :]).astype(bf16)
        scaled_out[ids[p], :, spans[p]] = scaled.T
        weights = unembedding[pl.ds(pl.multiple_of(ids[p] * width, width), width), :]
        accs[p] = jnp.dot(scaled, weights, preferred_element_type=f32)
        square = x * x
        total = square[:, :lanes]
        for start in range(lanes, width, lanes):
            total = total + square[:, start : start + lanes]
        sums[p] = total


def arrival_kernel(n, first, makes, exit_index, ring_size, step, *refs):
    ids = [block_index(ring_size, step - p, p == 1) for p in range(n)]
    pieces, refs = refs[:n], refs[n:]
    gain, unembedding = refs[:2]
    refs = refs[2:]
    if not first:
        acc, ss = refs[:2]
        refs = refs[2:]
    if not makes:
        refs = refs[1:]
    acc_out, ss_out, scaled_out = refs
    rows = pieces[0].shape[0]
    span = pl.ds(exit_index * rows, rows)
    accs, sums = [None] * n, [None] * n
    add_blocks(ids, pieces, [span] * n, gain, unembedding, accs, sums, scaled_out)
    total, squares = accs[0], sums[0]
    for p in range(1, n):
        total, squares = total + accs[p], squares + sums[p]
    if not first:
        total, squares = total + acc[...], squares + ss[...]
    acc_out[...] = total
    ss_out[...] = squares


def arrival(state, scaled, exit_index, exits, ring_size, step, pieces, gain, unembedding):
    rows, width = pieces[0].shape
    full, vocab = unembedding.shape
    lanes = min(128, width)
    n = len(pieces)
    first, makes = state is None, scaled is None
    args = [*pieces, gain, in_vmem(unembedding)]
    specs = [vmem_spec] * (n + 2)
    aliases = {}
    if not first:
        aliases = {len(args): 0, len(args) + 1: 1}
        args += list(state)
        specs += [vmem_spec, vmem_spec]
    if not makes:
        aliases[len(args)] = 2
        args.append(in_vmem(scaled))
        specs.append(vmem_spec)
    acc, ss, scaled = call(
        functools.partial(arrival_kernel, n, first, makes, exit_index, ring_size, step),
        "arrival",
        [
            jax.ShapeDtypeStruct((rows, vocab), f32),
            jax.ShapeDtypeStruct((rows, lanes), f32),
            pltpu.VMEM((full // width, width, exits * rows), bf16),
        ],
        specs,
        [vmem_spec, vmem_spec, vmem_spec],
        input_output_aliases=aliases,
    )(*args)
    return (acc, ss), scaled


def pull_kernel(ring_size, step, e, *refs):
    piece, gain, (own_out, relay_out) = refs[0], refs[1], refs[-2:]
    rows = piece.shape[0]
    owner, group = owner_index(ring_size, step), lax.axis_index("dp")

    @pl.when((owner >> 1) == (group >> 1))
    def _():
        block = owner * 2 + (lax.axis_index("vocab") & 1)
        x = piece[...].astype(f32) * gain[pl.ds(block, 1), :]
        turned = x.astype(bf16).T

        @pl.when(owner == group)
        def _():
            own_out[:, e * rows : (e + 1) * rows] = turned

        @pl.when(owner != group)
        def _():
            relay_out[:, e * rows : (e + 1) * rows] = turned


def pull(pulled, e, exits, ring_size, step, piece, gain):
    rows, width = piece.shape
    args = [piece, gain] + ([] if pulled is None else [in_vmem(x) for x in pulled])
    return call(
        functools.partial(pull_kernel, ring_size, step, e),
        "pull",
        [pltpu.VMEM((width, exits * rows), bf16)] * 2,
        [vmem_spec] * len(args),
        [vmem_spec] * 2,
        input_output_aliases={} if pulled is None else {2: 0, 3: 1},
    )(*args)


def target_mask(wanted, shape):
    first = (lax.axis_index("vocab") * shape[1]).astype(f32)
    return lax.broadcasted_iota(jnp.int32, shape, 1).astype(f32) + first == wanted


def split_kernel(a, b, first, second):
    count = first.shape[0]
    first[...] = a[:count, :]
    second[...] = b[count:, :]


def split_rows(a, b):
    rows, width = a.shape
    count = rows * 7 // 8
    shapes = [jax.ShapeDtypeStruct((n, width), a.dtype) for n in (count, rows - count)]
    return call(split_kernel, "split_rows", shapes, [vmem_spec] * 2, [vmem_spec] * 2)(a, b)


def last_kernel(e, full, ring_size, n, *refs):
    pieces, (gain, unembedding, old_acc, old_ss, targets) = refs[:n], refs[n : n + 5]
    logits_out, weights_out, stats_out, scaled_out = refs[-4:]
    rows = old_acc.shape[0]
    piece = jnp.concatenate([p[...] for p in pieces], axis=0) if n > 1 else pieces[0]
    span = pl.ds(e * rows, rows)
    accs, sums = [None], [None]
    ids = [block_index(ring_size, ring_size - 1, True)]
    add_blocks(ids, [piece], [span], gain, unembedding, accs, sums, scaled_out)
    square_sum = jnp.sum(old_ss[...] + sums[0], axis=1, keepdims=True)
    scale = lax.rsqrt(square_sum * (1.0 / full) + norm_eps)
    logits = (old_acc[...] + accs[0]) * scale
    logits_out[...] = logits
    wanted = jnp.broadcast_to(targets[...].astype(f32), (128, rows)).T[:, 0:1]
    hit = target_mask(wanted, logits.shape)
    target = jnp.sum(jnp.where(hit, logits, 0.0), axis=1, keepdims=True)
    top = jnp.max(logits, axis=1, keepdims=True)
    weights = jnp.exp(logits - top)
    weights_out[span, :] = weights.astype(bf16)
    total = jnp.sum(weights, axis=1, keepdims=True)
    lane = lax.broadcasted_iota(jnp.int32, (rows, 128), 1)
    packed = jnp.where(
        lane == 0, top, jnp.where(lane == 1, total, jnp.where(lane == 2, target, scale))
    )
    packed = jnp.where(lane == 4, wanted, jnp.where(lane == 5, top, packed))
    stats_out[:, e * rows : (e + 1) * rows] = packed.T[:8, :]


def last_block(e, exits, made, state, scaled, ring_size, pieces, targets, gain, unembedding):
    rows = state[0].shape[0]
    full, vocab = unembedding.shape
    args = [*pieces, gain, in_vmem(unembedding), *state, targets]
    args += [*made, in_vmem(scaled)]
    n = len(args)
    aliases = {n - 1: 3, n - 2: 2, n - 3: 1} if made else {n - 1: 3}
    return call(
        functools.partial(last_kernel, e, full, ring_size, len(pieces)),
        "last_block",
        [
            jax.ShapeDtypeStruct((rows, vocab), f32),
            jax.ShapeDtypeStruct((exits * rows, vocab), bf16),
            jax.ShapeDtypeStruct((8, exits * rows), f32),
            pltpu.VMEM(scaled.shape, bf16),
        ],
        [vmem_spec] * n,
        [vmem_spec] * 4,
        input_output_aliases=aliases,
    )(*args)


def merge_kernel(n, *refs):
    out = refs[-1]
    rows = refs[0].shape[1]
    for k in range(n):
        a, b = refs[2 * k], refs[2 * k + 1]
        top_a, top_b = a[0:1, :], b[0:1, :]
        top = jnp.maximum(top_a, top_b)
        total = a[1:2, :] * jnp.exp(top_a - top) + b[1:2, :] * jnp.exp(top_b - top)
        target = a[2:3, :] + b[2:3, :]
        row = lax.broadcasted_iota(jnp.int32, (out.shape[0], rows), 0)
        merged = jnp.where(row == 0, top, jnp.where(row == 1, total, target))
        merged = jnp.where(row > 2, a[...], merged)
        out[:, k * rows : (k + 1) * rows] = merged


def merge(*pairs):
    rows = pairs[0][0].shape[1]
    shape = jax.ShapeDtypeStruct((8, len(pairs) * rows), f32)
    kernel = functools.partial(merge_kernel, len(pairs))
    args = [x for pair in pairs for x in pair]
    return call(kernel, "merge_stats", shape, [vmem_spec] * len(args), vmem_spec)(*args)


def exit_rows(e, rows, stats, exit_scale):
    cols = slice(e * rows, (e + 1) * rows)
    weight = exit_scale[0:1, e : e + 1]
    log_total = stats[0:1, cols] + jnp.log(stats[1:2, cols])
    target = stats[2:3, cols]
    loss = weight * jnp.sum(log_total - target, axis=1, keepdims=True)
    return log_total, target, stats[3:4, cols] * weight, loss


def turn(rows, first, second, third):
    row = lax.broadcasted_iota(jnp.int32, (128, rows), 0)
    turned = jnp.where(row == 0, first, jnp.where(row == 1, second, third)).T
    return turned[:, 0:1], turned[:, 1:2], turned[:, 2:3]


def exit_grads(e, values, stats, exit_scale):
    rows = values.shape[0]
    log_total, _, factor, loss = exit_rows(e, rows, stats, exit_scale)
    wanted = stats[4:5, e * rows : (e + 1) * rows]
    log_total, factor, wanted = turn(rows, log_total, factor, wanted)
    hit = target_mask(wanted, values.shape)
    soft = jnp.exp(values - log_total) - jnp.where(hit, 1.0, 0.0)
    return (soft * factor).astype(bf16), loss


def exit_grads_of(e, weights, stats, exit_scale):
    rows = weights.shape[0]
    log_total, target, factor, loss = exit_rows(e, rows, stats, exit_scale)
    cols = slice(e * rows, (e + 1) * rows)
    others = jnp.exp(stats[5:6, cols] - log_total) * factor
    at_target = (jnp.exp(target - log_total) - 1.0) * factor
    others, at_target, wanted = turn(rows, others, at_target, stats[4:5, cols])
    hit = target_mask(wanted, weights.shape)
    return jnp.where(hit, at_target, weights.astype(f32) * others).astype(bf16), loss


def grad_kernel(exits, paired, *refs):
    logits, (stats, exit_scale, *scaled, grad_out, loss_out) = refs[:exits], refs[exits : len(refs) - bool(paired)]
    rows = logits[0].shape[0]
    total = jnp.zeros((1, 1), f32)
    for e in range(exits):
        grads, loss = exit_grads(e, logits[e][...], stats, exit_scale)
        grad_out[e * rows : (e + 1) * rows, :] = grads
        total = total + loss
    loss_out[...] = jnp.broadcast_to(total, loss_out.shape)
    if paired:
        group = lax.axis_index("dp")
        share = ((group >> 1) ^ 1) * 2 + 1 - (group & 1)
        block = share * 2 + 1 - (lax.axis_index("vocab") & 1)
        away = jnp.dot(scaled[0][block], grad_out[...], preferred_element_type=f32)
        refs[-1][...] = away.astype(bf16)


def row_grads(logits, stats, exit_scale, scaled):
    exits = len(logits)
    rows, vocab = logits[0].shape
    shapes = [jax.ShapeDtypeStruct((exits * rows, vocab), bf16), jax.ShapeDtypeStruct((8, 128), f32)]
    args = [*logits, stats, exit_scale]
    if scaled is not None:
        shapes.append(jax.ShapeDtypeStruct((scaled.shape[1], vocab), bf16))
        args.append(in_vmem(scaled))
    return call(
        functools.partial(grad_kernel, exits, scaled is not None),
        "row_grads",
        shapes,
        [vmem_spec] * len(args),
        [vmem_spec] * len(shapes),
    )(*args)


def block_kernel(has_added, high_flip, away, units, unit, scaled, grads, *refs):
    out = refs[-1]
    group = lax.axis_index("dp")
    low = group & 1
    share = ((group >> 1) ^ high_flip) * 2 + (1 - low if away else low)
    if unit == "crossed":
        unit = 1 - (lax.axis_index("vocab") & 1)
    elif unit == "own":
        unit = lax.axis_index("vocab") & 1
    block = share * units + unit
    total = jnp.dot(scaled[block], grads[...], preferred_element_type=f32)
    if has_added:
        total = total + refs[0][...].astype(f32)
    out[...] = total.astype(out.dtype)


def grad_block(high_flip, away, units, unit, scaled, grads, added, dtype):
    width, vocab = scaled.shape[1], grads.shape[1]
    args = [in_vmem(scaled), grads] + ([] if added is None else [added])
    return call(
        functools.partial(block_kernel, added is not None, high_flip, away, units, unit),
        "grad_block",
        jax.ShapeDtypeStruct((width, vocab), dtype),
        [vmem_spec] * len(args),
        vmem_spec,
    )(*args)


def sum_kernel(units, tiles, n, count, *refs):
    parts, (loss, other, out, mean, buf, sems) = refs[: n * units], refs[n * units :]
    mean[...] = (loss[0:1, 0:1] + other[0:1, 0:1]) * (1.0 / count)
    height = parts[0].shape[0]
    tile = height // tiles
    copies = []
    for unit in range(units):
        for t in range(tiles):
            span = slice(t * tile, (t + 1) * tile)
            to = pl.ds(unit * height + t * tile, tile)
            total = parts[unit][span, :]
            for k in range(1, n):
                total = total + parts[k * units + unit][span, :].astype(f32)
            buf[to, :] = total
            copies.append(
                pltpu.make_async_copy(buf.at[to], out.at[to], sems.at[unit * tiles + t])
            )
            copies[-1].start()
    for copy in copies:
        copy.wait()


def sum_units(lists, loss, other, count):
    units = len(lists[0])
    height, vocab = lists[0][0].shape
    tiles = max(1, height // 256)
    return call(
        functools.partial(sum_kernel, units, tiles, len(lists), count),
        "sum_units",
        [
            jax.ShapeDtypeStruct((units * height, vocab), f32),
            jax.ShapeDtypeStruct((1, 1), f32),
        ],
        [vmem_spec] * (units * len(lists) + 2),
        [hbm_spec, vmem_spec],
        scratch_shapes=[
            pltpu.VMEM((units * height, vocab), f32),
            pltpu.SemaphoreType.DMA((units * tiles,)),
        ],
    )(*[part for parts in lists for part in parts], loss, other)


def own_kernel(exits, count, *refs):
    weights, refs = refs[:2], refs[2:]
    stats, refs = refs[:2], refs[2:]
    exit_scale, *pulled, scaled, grads, came, loss, loss_core = refs[:8]
    out, part, mean, buf, sem = refs[8:]
    rows = weights[0].shape[0] // exits
    height = buf.shape[0]
    side = lax.axis_index("vocab") & 1
    block = lax.axis_index("dp") * 2
    total = jnp.dot(scaled[block + side], grads[...], preferred_element_type=f32)
    total = total + came[pl.ds(pl.multiple_of(side * height, height), height), :].astype(f32)
    total_loss = loss[0:1, 0:1] + loss_core[0:1, 0:1]
    for k in range(2):
        for e in range(exits):
            values = weights[k][e * rows : (e + 1) * rows, :]
            other, loss_part = exit_grads_of(e, values, stats[k], exit_scale)
            total_loss = total_loss + loss_part
            rows_of = pulled[k][:, e * rows : (e + 1) * rows]
            total = total + jnp.dot(rows_of, other, preferred_element_type=f32)
    buf[...] = total
    to = pl.ds(pl.multiple_of(side * height, height), height)
    copy = pltpu.make_async_copy(buf, out.at[to], sem)
    copy.start()
    mean[...] = total_loss * (1.0 / count)
    crossed = jnp.dot(scaled[block + 1 - side], grads[...], preferred_element_type=f32)
    other_side = pl.multiple_of((1 - side) * height, height)
    part[...] = crossed + came[pl.ds(other_side, height), :].astype(f32)
    copy.wait()


def away_kernel(scaled, grads, out):
    group = lax.axis_index("dp")
    block = ((group >> 1) * 2 + 1 - (group & 1)) * 2
    width = scaled.shape[1]
    for unit in range(2):
        part = jnp.dot(scaled[block + unit], grads[...], preferred_element_type=f32)
        out[unit * width : (unit + 1) * width, :] = part.astype(bf16)


def away_share(scaled, grads):
    width, vocab = scaled.shape[1], grads.shape[1]
    shape = jax.ShapeDtypeStruct((2 * width, vocab), bf16)
    return call(away_kernel, "away_share", shape, [vmem_spec] * 2, vmem_spec)(in_vmem(scaled), grads)


def own_block(weights, stats, exit_scale, pulled, scaled, grads, came, losses, count):
    exits = exit_scale.shape[1]
    height, vocab = came.shape[0] // 2, came.shape[1]
    args = [*weights, *stats, exit_scale, *pulled, in_vmem(scaled), grads, came, *losses]
    return call(
        functools.partial(own_kernel, exits, count),
        "own_block",
        [
            jax.ShapeDtypeStruct((2 * height, vocab), f32),
            jax.ShapeDtypeStruct((height, vocab), f32),
            jax.ShapeDtypeStruct((1, 1), f32),
        ],
        [vmem_spec] * len(args),
        [hbm_spec, vmem_spec, vmem_spec],
        scratch_shapes=[pltpu.VMEM((height, vocab), f32), pltpu.SemaphoreType.DMA],
    )(*args)


def crossed_kernel(tiles, part, over, _, out, buf, sems):
    height = part.shape[0]
    tile = height // tiles
    start = (1 - (lax.axis_index("vocab") & 1)) * height
    copies = []
    for t in range(tiles):
        span = slice(t * tile, (t + 1) * tile)
        buf[span, :] = part[span, :] + over[span, :].astype(f32)
        to = pl.ds(pl.multiple_of(start + t * tile, tile), tile)
        copies.append(pltpu.make_async_copy(buf.at[pl.ds(t * tile, tile)], out.at[to], sems.at[t]))
        copies[t].start()
    for copy in copies:
        copy.wait()


def crossed_block(part, over, out):
    height, vocab = part.shape
    tiles = max(1, height // 256)
    return call(
        functools.partial(crossed_kernel, tiles),
        "crossed_block",
        jax.ShapeDtypeStruct(out.shape, f32),
        [vmem_spec, vmem_spec, hbm_spec],
        hbm_spec,
        input_output_aliases={2: 0},
        scratch_shapes=[pltpu.VMEM((height, vocab), f32), pltpu.SemaphoreType.DMA((tiles,))],
    )(part, over, out)


def flip(axis, bit):
    return [(i, i ^ bit) for i in range(lax.axis_size(axis))]


def per_device(hidden_states, exit_layers, targets, norm_gain, exit_scale, unembedding):
    exits = exit_layers.shape[1]
    tokens = hidden_states.shape[1]
    full, vocab_local = unembedding.shape
    n_vocab, n_dp = lax.axis_size("vocab"), lax.axis_size("dp")
    ring_size = n_vocab // 2
    ring = [(j, (j + 2) % n_vocab) for j in range(n_vocab)]
    pair = flip("vocab", 1)
    layers = exit_layers.T
    gain = norm_gain.astype(f32).reshape(n_vocab, full // n_vocab)
    target_row = targets.reshape(1, tokens)

    paired = n_dp == 4 and n_vocab == 2 * n_dp

    def pull_pairs(step):
        pairs = []
        for d in range(n_dp):
            for j in range(n_vocab):
                if (j // 2 - step) % ring_size // 2 != d // 2:
                    pairs.append((d * n_vocab + j, (d ^ 2) * n_vocab + j))
        return pairs

    states, scaled = [None] * exits, None
    current = [select(hidden_states, layers, e) for e in range(exits)]
    crossed, pulled, pending = None, None, None
    for step in range(ring_size):
        last = step == ring_size - 1
        crossing, coming = [], []
        for e in range(exits):
            piece = current[e]
            if crossed is not None:
                before = (e - 1) % exits
                piece, crossed[e], states[before] = bar((piece, crossed[e], states[before]))
            elif e:
                piece, states[e - 1] = bar((piece, states[e - 1]))
            if not last:
                coming.append(lax.ppermute(piece, "vocab", ring))
            if last and step > 0 and e >= exits // 2:
                from_ring, from_pair = split_rows(crossed[e], piece)
                crossing.append(
                    [lax.ppermute(from_ring, "vocab", ring), lax.ppermute(from_pair, "vocab", pair)]
                )
            else:
                crossed_piece = lax.ppermute(piece, "vocab", pair)
                crossing.append([crossed_piece] if last else crossed_piece)
            sent = lax.ppermute(piece, ("dp", "vocab"), pull_pairs(step)) if paired else None
            if pending is not None:
                piece, came = bar((piece, pending[2]))
                pulled = pull(pulled, pending[1], exits, ring_size, pending[0], came, gain)
            pending = (step, e, sent) if paired else None
            if last and e:
                piece, crossing[0] = bar((piece, crossing[0]))
            pieces = [piece] if crossed is None else [piece, crossed[e]]
            states[e], scaled = arrival(
                states[e], scaled, e, exits, ring_size, step, pieces, gain, unembedding
            )
        crossed, current = crossing, coming

    def over_y(x):
        return lax.ppermute(x, "dp", flip("dp", 2))

    def over_core(x):
        return lax.ppermute(x, "dp", flip("dp", 1))

    logits, made = [], ()
    for e in range(exits):
        values, *made, scaled = last_block(
            e, exits, made, states[e], scaled, ring_size, crossed[e], target_row, gain, unembedding
        )
        logits.append(values)
    weights, stats = made
    stats = merge((stats, lax.ppermute(stats, "vocab", pair)))
    scale_row = exit_scale.reshape(1, exits)
    if paired:
        weights, stats = bar((weights, stats))
        y_weights = over_y(weights)
    bit = 2
    while bit < n_vocab:
        if 2 * bit == n_vocab and paired:
            stats, came, pulled = bar((stats, pending[2], pulled))
        stats = merge((stats, lax.ppermute(stats, "vocab", flip("vocab", bit))))
        bit *= 2
    if paired:
        stats, y_weights = bar((stats, y_weights))
        y_stats = over_y(stats)
        pulled = pull(pulled, pending[1], exits, ring_size, pending[0], came, gain)
        y_weights, pulled = bar((y_weights, pulled, stats))[:2]
        yc_weights = over_core(y_weights)
        pulled = (pulled[0], over_core(pulled[1]))
    grads, loss, *away = row_grads(logits, stats, scale_row, scaled if paired else None)

    if paired:
        came = over_core(away[0])
        came, share = bar((came, away_share(scaled, grads)))
        home = grad_block(1, False, 2, "crossed", scaled, grads, came, bf16)
        over = over_y(home)
        share, y_stats = bar((share, y_stats))
        came = over_core(share)
        weight_grad, part, mean_loss = own_block(
            (y_weights, yc_weights), (y_stats, over_core(y_stats)), scale_row,
            pulled, scaled, grads, came, (loss, over_core(loss)), tokens * n_dp,
        )
        return (crossed_block(part, over, weight_grad), mean_loss.reshape(()))

    n_high = n_dp // 2
    units = n_vocab // n_dp
    held = {}
    for high_flip in reversed(range(n_high)):
        came = []
        for unit in range(units):
            away = grad_block(high_flip, True, units, unit, scaled, grads, None, bf16)
            came.append(lax.ppermute(away, "dp", flip("dp", 1)))
        for unit in range(units):
            held[high_flip, unit] = grad_block(
                high_flip, False, units, unit, scaled, grads,
                came[unit] if high_flip else None, bf16 if high_flip else f32,
            )
        if high_flip:
            grads, loss = bar((grads, loss, *[held[high_flip, unit] for unit in range(units)]))[:2]
    bit = 1
    while bit < n_high:
        loss = loss + lax.ppermute(loss, "dp", flip("dp", bit))
        bit *= 2
    other_loss = lax.ppermute(loss, "dp", flip("dp", bit))
    bit = 1
    while bit < n_high:
        kept = {}
        for h in reversed(range(0, n_high, 2 * bit)):
            over = [
                lax.ppermute(held[h + bit, unit], "dp", flip("dp", 2 * bit)) for unit in range(units)
            ]
            if 2 * bit == n_high:
                parts = [[held[0, unit] for unit in range(units)], came, over]
                weight_grad, mean_loss = sum_units(parts, loss, other_loss, tokens * n_dp)
            else:
                for unit in range(units):
                    total = held[h, unit].astype(f32) + over[unit].astype(f32)
                    kept[h, unit] = total.astype(bf16) if h else total
        held = kept
        bit *= 2
    return (weight_grad, mean_loss.reshape(()))


def solution(mesh):
    in_specs = (P(None, "dp", "vocab"), P("dp", None), P("dp"), P(), P(), P(None, "vocab"))
    out_specs = (P("dp", "vocab"), P())
    return jax.shard_map(
        per_device, mesh=mesh, in_specs=in_specs, out_specs=out_specs, check_vma=False
    )
```
